32 devices in a mesh: blk: 8 (over y, x, core), grp: 4 (over z).
Axes of the slice: x: 2, y: 2, z: 4, core: 2. Of those that a mesh axis runs over, the one named last changes fastest.
Arguments:
- tensor_blocks: bfloat16 [1152, 64, 4096], P(('blk', 'grp')), may hold values from 0 to 1
- block_coords: int32 [3, 1152], P(None, ('blk', 'grp')), may hold values from 0 to 63, as said below
- block_count: int32 [32], P(('blk', 'grp')), may hold values from 1 to 36, as said below
- row_owner: int32 [3, 64], replicated, may hold values from 0 to 63, as said below
- factors: float32 [3, 4096, 256], P(None, ('blk', 'grp')), may hold values from -2.4 to 2.4
- moment1: float32 [4096, 256], P(('blk', 'grp')), may hold values from -1.8 to 1.8
- moment2: float32 [4096, 256], P(('blk', 'grp')), may hold values from 0.01 to 1
Outputs:
- new_factor: float32 [4096, 256], P(('blk', 'grp'))
- new_moment1: float32 [4096, 256], P(('blk', 'grp'))
- new_moment2: float32 [4096, 256], P(('blk', 'grp'))
The draws below stay inside these ranges and needn't reach their ends.
Inputs may be any that keep to these rules, and one draw needn't show every extreme that they name: `row_owner`: for each mode a permutation; storage position p lies on device p // 2 of blk+grp. `block_coords`: of the 108 row blocks named by one device's slots, at most 5 have positions on any one device, and exactly 5 on some device; of the 36 first-mode row blocks named by one device's slots, at most 2 have positions on any one device, and exactly 2 on some device. `block_count`: some device has all slots live.
All inputs are finite; a program needn't handle non-finite values.
Results may differ from the reference program's by a relative error of at most 0.0012.
Values may be sent and summed in bfloat16 or wider, within the bound.
No kernel may reach another device: no remote copies, remote signals or barrier semaphores. Data moves between devices by JAX's collectives and lax.ppermute only.
A program may use at most 128 MiB of HBM per device.

```python
import math
import jax
import jax.numpy as jnp
from jax import lax

E = 64
R = 256
BLK_DEV = 36
ROWB = 2
NBLK = 1152
NROWB = 64
ROWS = 4096
CAP = 5
CAP0 = 2
DEVICES = 32


def common_tables(key):
    perms = jnp.stack([jax.random.permutation(jax.random.fold_in(key, 11 + m), NROWB) for m in range(3)]).astype(jnp.int32)
    inverse = jnp.argsort(perms, axis=1).astype(jnp.int32)
    spread = DEVICES * CAP

    def one_device(device):
        base = jax.random.fold_in(jax.random.fold_in(key, 29), device)
        key_first, key_pool, key_order, key_slot, key_score, key_rest = jax.random.split(base, 6)
        first = jax.random.randint(key_first, (), 0, DEVICES)
        pool = (first + 1 + jnp.repeat(jnp.arange(DEVICES - 1), CAP0)) % DEVICES
        pool = jax.random.permutation(key_pool, pool)[:BLK_DEV - CAP0]
        dests_first = jnp.concatenate([jnp.full((CAP0,), first, jnp.int32), pool.astype(jnp.int32)])
        dests_first = jax.random.permutation(key_order, dests_first).astype(jnp.int32)
        counts_first = jnp.sum((dests_first[:, None] == jnp.arange(DEVICES)[None, :]).astype(jnp.int32), axis=0)
        cand_dev = jnp.repeat(jnp.arange(DEVICES, dtype=jnp.int32), CAP)
        cand_rank = jnp.tile(jnp.arange(CAP, dtype=jnp.int32), DEVICES)
        valid = cand_rank >= jnp.take(counts_first, cand_dev)
        scores = jax.random.permutation(key_score, spread).astype(jnp.int32)
        scores = jnp.where(valid, scores, scores + 2 * spread)
        scores = jnp.where(valid & (cand_dev == first), scores - 2 * spread, scores)
        chosen = jnp.take(cand_dev, jnp.argsort(scores)[:2 * BLK_DEV])
        chosen = jax.random.permutation(key_rest, chosen).astype(jnp.int32)
        dests = jnp.concatenate([dests_first, chosen])
        slot = jax.random.randint(key_slot, (3 * BLK_DEV,), 0, ROWB)
        return (dests * ROWB + slot).astype(jnp.int32)
    spots = jax.vmap(one_device)(jnp.arange(DEVICES))
    spots = spots.reshape(DEVICES, 3, BLK_DEV).transpose(1, 0, 2).reshape(3, NBLK)
    coords = jnp.take_along_axis(inverse, spots, axis=1)
    return (perms, coords)


def draw_row_owner(key, part):
    return common_tables(key)[0]


def draw_block_coords(key, part):
    return common_tables(key)[1]


def draw_block_count(key, part):
    key_counts, key_full = jax.random.split(jax.random.fold_in(key, 53))
    counts = jax.random.randint(key_counts, (DEVICES,), max(1, BLK_DEV // 4), BLK_DEV + 1)
    fullest = jax.random.randint(key_full, (), 0, DEVICES)
    return counts.at[fullest].set(BLK_DEV).astype(jnp.int32)


def level_of(rng, extent, pieces, smallest, high):
    def one(axis_at, parts):
        draws = jax.random.uniform(jax.random.fold_in(jax.random.fold_in(rng, 6), axis_at), (parts,), jnp.float32, smallest / len(pieces), high / len(pieces))
        return jnp.repeat(jnp.exp(draws), extent[axis_at] // parts).reshape((-1,) + (1,) * (len(extent) - axis_at - 1))

    factor_of = one(*pieces[0])
    for cut in pieces[1:]:
        factor_of = factor_of * one(*cut)
    return factor_of


def normal_values(stream_key, shape, width, bound, pieces=(), held_as=jnp.bfloat16):
    entries = width * jax.random.normal(stream_key, shape, jnp.float32)
    if pieces:
        entries = entries * level_of(stream_key, shape, pieces, -0.22, 0.18)
    return jnp.clip(entries, -bound, bound).astype(held_as)


def setup_inputs(seed: int = 0) -> dict:
    streams_of = jax.random.split(jax.random.key(seed), 8)
    return {
        "tensor_blocks": jnp.clip(1.0 * jax.random.uniform(streams_of[0], (NBLK, E, E * E), jnp.float32) ** level_of(streams_of[0], (NBLK, E, E * E), ((0, 32),), -0.2, 0.2), 0.0, 1.0).astype(jnp.bfloat16),
        "block_coords": draw_block_coords(jax.random.fold_in(streams_of[7], 71), 0),
        "block_count": draw_block_count(jax.random.fold_in(streams_of[7], 71), 0),
        "row_owner": draw_row_owner(jax.random.fold_in(streams_of[7], 71), 0),
        "factors": normal_values(streams_of[4], (3, ROWS, R), 0.4, 2.4, ((1, 32),), jnp.float32),
        "moment1": normal_values(streams_of[5], (ROWS, R), 0.3, 1.8, ((0, 32),), jnp.float32),
        "moment2": jnp.clip(jnp.exp(math.log(1.0) - 4.6051702 * jax.random.uniform(streams_of[6], (ROWS, R), jnp.float32) ** level_of(streams_of[6], (ROWS, R), ((0, 32),), -0.2, 0.2)), 0.01, 1.0),
    }


def reference(tensor_blocks, block_coords, block_count, row_owner, factors, moment1, moment2):
    nblk = tensor_blocks.shape[0]
    slots = jnp.arange(nblk, dtype=jnp.int32)
    counts = jnp.take(block_count, slots // BLK_DEV)
    live = (slots % BLK_DEV < counts).astype(jnp.float32)
    positions = jnp.stack([jnp.take(row_owner[m], block_coords[m]) for m in range(3)], axis=1).astype(jnp.int32)

    def step(grad, item):
        block, pos, alive = item
        rows = [lax.dynamic_slice_in_dim(factors[m], (pos[m] * E).astype(jnp.int32), E, 0).astype(jnp.bfloat16) for m in range(3)]
        pair = (rows[1].astype(jnp.float32)[:, None, :] * rows[2].astype(jnp.float32)[None, :, :]).reshape(E * E, R).astype(jnp.bfloat16)
        model = lax.dot_general(rows[0], pair, (((1,), (1,)), ((), ())), preferred_element_type=jnp.float32)
        resid = ((jax.nn.sigmoid(model) - block.astype(jnp.float32)) * alive).astype(jnp.bfloat16)
        part = jnp.dot(resid, pair, preferred_element_type=jnp.float32)
        start = (pos[0] * E).astype(jnp.int32)
        old = lax.dynamic_slice_in_dim(grad, start, E, 0)
        return (lax.dynamic_update_slice_in_dim(grad, old + part, start, 0), None)
    grad, _ = lax.scan(step, jnp.zeros((ROWS, R), jnp.float32), (tensor_blocks, positions, live))
    new_moment1 = 0.9 * moment1 + 0.1 * grad
    new_moment2 = 0.999 * moment2 + 0.001 * grad * grad
    new_factor = factors[0] - 0.02 * (new_moment1 / (1.0 - 0.9 ** 8)) / (jnp.sqrt(new_moment2 / (1.0 - 0.999 ** 8)) + 1e-08)
    return (new_factor, new_moment1, new_moment2)
```

```python
import functools

import jax
import jax.numpy as jnp
from jax import lax
from jax.experimental import pallas as pl
from jax.experimental.pallas import tpu as pltpu
from jax.sharding import PartitionSpec as P

AXES = ("blk", "grp")
BUFFERS = 3
TILE_J = 4


def slots_kernel(
    local_blocks,
    coords_ref,
    count_ref,
    owner_ref,
    blocks_ref,
    table_ref,
    grad_ref,
    blocks_buf,
    rows_buf,
    block_sems,
    row_sems,
):
    edge, rank = rows_buf.shape[2], rows_buf.shape[3]
    count = count_ref[0]
    grad_ref[...] = jnp.zeros_like(grad_ref)

    def copies(slot):
        at = lax.rem(slot, BUFFERS)
        out = [pltpu.make_async_copy(blocks_ref.at[slot], blocks_buf.at[at], block_sems.at[at])]
        for mode in range(3):
            pos = owner_ref[mode, coords_ref[mode, slot]]
            device = lax.div(pos, local_blocks)
            place = (device * 3 + mode) * local_blocks + lax.rem(pos, local_blocks)
            out.append(
                pltpu.make_async_copy(
                    table_ref.at[place], rows_buf.at[at, mode], row_sems.at[at, mode]
                )
            )
        return out

    def start(slot):
        @pl.when(slot < count)
        def _():
            for copy in copies(slot):
                copy.start()

    for slot in range(BUFFERS - 1):
        start(slot)

    def step(slot, carry):
        start(slot + BUFFERS - 1)
        for copy in copies(slot):
            copy.wait()
        at = lax.rem(slot, BUFFERS)
        rows_a = rows_buf[at, 0] * jnp.asarray(0.5, jnp.bfloat16)
        rows_c = rows_buf[at, 2]
        width = TILE_J * edge
        tiles = edge // TILE_J

        def pair_of(tile):
            return jnp.concatenate(
                [
                    rows_buf[at, 1, pl.ds(tile * TILE_J + j, 1), :] * rows_c
                    for j in range(TILE_J)
                ],
                axis=0,
            )

        def half_model(pair):
            return lax.dot_general(
                rows_a, pair, (((1,), (1,)), ((), ())), preferred_element_type=jnp.float32
            )

        total = jnp.zeros((edge, rank), jnp.float32)
        pair = pair_of(0)
        model = half_model(pair)
        for tile in range(tiles):
            if tile + 1 < tiles:
                next_pair = pair_of(tile + 1)
                next_model = half_model(next_pair)
            twice = blocks_buf[at, :, tile * width : (tile + 1) * width].astype(jnp.float32) * 2.0
            resid = ((jnp.tanh(model) + 1.0) - twice).astype(jnp.bfloat16)
            total = total + jnp.dot(resid, pair, preferred_element_type=jnp.float32)
            if tile + 1 < tiles:
                pair, model = next_pair, next_model
        target = owner_ref[0, coords_ref[0, slot]]
        grad_ref[target] += 0.5 * total
        return carry

    lax.fori_loop(0, count, step, 0)


def per_device(tensor_blocks, block_coords, block_count, row_owner, factors, moment1, moment2):
    slot_count, edge, width = tensor_blocks.shape
    rank = factors.shape[2]
    local_blocks = moment1.shape[0] // edge
    row_blocks = row_owner.shape[1]
    shard = factors.astype(jnp.bfloat16).reshape(3 * local_blocks, edge, rank)
    table = lax.all_gather(shard, AXES, axis=0, tiled=True)
    smem = pl.BlockSpec(memory_space=pltpu.SMEM)
    hbm = pl.BlockSpec(memory_space=pl.ANY)
    flops = 4 * slot_count * edge * width * rank
    grads = pl.pallas_call(
        functools.partial(slots_kernel, local_blocks),
        out_shape=jax.ShapeDtypeStruct((row_blocks, edge, rank), jnp.float32),
        in_specs=[smem, smem, smem, hbm, hbm],
        out_specs=pl.BlockSpec(memory_space=pltpu.VMEM),
        scratch_shapes=[
            pltpu.VMEM((BUFFERS, edge, width), jnp.bfloat16),
            pltpu.VMEM((BUFFERS, 3, edge, rank), jnp.bfloat16),
            pltpu.SemaphoreType.DMA((BUFFERS,)),
            pltpu.SemaphoreType.DMA((BUFFERS, 3)),
        ],
        compiler_params=pltpu.CompilerParams(vmem_limit_bytes=48 * 1024 * 1024),
        cost_estimate=pl.CostEstimate(
            flops=flops,
            bytes_accessed=2 * slot_count * edge * width,
            transcendentals=slot_count * edge * width,
        ),
    )(block_coords, block_count, row_owner, tensor_blocks, table)
    grad = lax.psum_scatter(
        grads.reshape(row_blocks * edge, rank), AXES, scatter_dimension=0, tiled=True
    )
    new_moment1 = 0.9 * moment1 + 0.1 * grad
    new_moment2 = 0.999 * moment2 + 0.001 * grad * grad
    new_factor = factors[0] - 0.02 * (new_moment1 / (1.0 - 0.9**8)) / (
        jnp.sqrt(new_moment2 / (1.0 - 0.999**8)) + 1e-08
    )
    return (new_factor, new_moment1, new_moment2)


def solution(mesh):
    return jax.shard_map(
        per_device,
        mesh=mesh,
        in_specs=(
            P(AXES, None, None),
            P(None, AXES),
            P(AXES),
            P(),
            P(None, AXES, None),
            P(AXES, None),
            P(AXES, None),
        ),
        out_specs=(P(AXES, None), P(AXES, None), P(AXES, None)),
        check_vma=False,
    )
```

```python
import functools

import jax
import jax.numpy as jnp
from jax import lax
from jax.experimental import pallas as pl
from jax.experimental.pallas import tpu as pltpu
from jax.sharding import PartitionSpec as P

AXES = ("blk", "grp")
CORES = 2
BUFFERS = 4
AHEAD = 2
TILE_J = 4
LAG = 2


def mesh_dims(blk, grp):
    chips = blk // CORES
    inner = 1
    for width in range(1, chips + 1):
        if chips % width == 0 and width * width <= chips:
            inner = width
    return {"outer": chips // inner, "inner": inner, "core": CORES, "line": grp}


def split_index(index, dims):
    line = lax.rem(index, dims["line"])
    rest = lax.div(index, dims["line"])
    core = lax.rem(rest, dims["core"])
    rest = lax.div(rest, dims["core"])
    return {
        "outer": lax.div(rest, dims["inner"]),
        "inner": lax.rem(rest, dims["inner"]),
        "core": core,
        "line": line,
    }


def shift(values, dims, name, step):
    strides = {
        "line": 1,
        "core": dims["line"],
        "inner": dims["line"] * dims["core"],
        "outer": dims["line"] * dims["core"] * dims["inner"],
    }
    total = strides["outer"] * dims["outer"]
    stride, size = strides[name], dims[name]
    perm = []
    for source in range(total):
        at = source // stride % size
        perm.append((source, source + ((at + step) % size - at) * stride))
    return lax.ppermute(values, AXES, perm)


ORDERS = (("outer", "inner"), ("inner", "outer"))


def gather_rows(shard, dims):
    count = shard.shape[0]
    cut = count // 2
    line = [shard] + [shift(shard, dims, "line", k) for k in range(1, dims["line"])]
    halves = []
    for part, (first, second) in zip((slice(0, cut), slice(cut, count)), ORDERS):
        own = jnp.concatenate([piece[part] for piece in line])
        own = jnp.concatenate([own] + [shift(own, dims, first, k) for k in range(1, dims[first])])
        pieces = [own] + [shift(own, dims, second, k) for k in range(1, dims[second])]
        pieces = pieces + [shift(piece, dims, "core", 1) for piece in pieces]
        halves.append(pieces)
    return halves


def slots_kernel(dims, local_blocks, piece_count, *refs):
    coords_ref, count_ref, owner_ref, blocks_ref = refs[:4]
    pieces = refs[4 : 4 + piece_count]
    (
        mine_ref,
        other_ref,
        table_ref,
        grad_ref,
        blocks_buf,
        pair_ref,
        model_ref,
        total_ref,
        block_sems,
        piece_sems,
        out_sems,
    ) = refs[4 + piece_count :]
    edge, rank = grad_ref.shape[1], grad_ref.shape[2]
    width = TILE_J * edge
    tiles = edge // TILE_J
    count = count_ref[0]
    cut = 3 * local_blocks // 2
    here = split_index(lax.axis_index("blk") * dims["line"] + lax.axis_index("grp"), dims)
    columns = dims["core"] * dims["outer"] * dims["inner"] * dims["line"]

    def row_place(mode, slot):
        pos = owner_ref[mode, coords_ref[mode, slot]]
        there = split_index(lax.div(pos, local_blocks), dims)
        away = {
            name: lax.rem(here[name] - there[name] + dims[name], dims[name]) for name in dims
        }
        block = mode * local_blocks + lax.rem(pos, local_blocks)
        late = block >= cut
        second = jnp.where(late, away["outer"], away["inner"])
        first = jnp.where(late, away["inner"], away["outer"])
        size_first = jnp.where(late, dims["inner"], dims["outer"])
        size_second = jnp.where(late, dims["outer"], dims["inner"])
        spot = ((away["core"] * size_second + second) * size_first + first) * dims["line"]
        spot = spot + away["line"]
        blocks_of = jnp.where(late, 3 * local_blocks - cut, cut)
        base = jnp.where(late, columns * cut, 0)
        return base + spot * blocks_of + jnp.where(late, block - cut, block)

    def grad_place(slot):
        pos = owner_ref[0, coords_ref[0, slot]]
        there = split_index(lax.div(pos, local_blocks), dims)
        away = {
            name: lax.rem(there[name] - here[name] + dims[name], dims[name]) for name in dims
        }
        local = lax.rem(pos, local_blocks)
        half_blocks = local_blocks // 2
        late = local >= half_blocks
        second = jnp.where(late, away["outer"], away["inner"])
        first = jnp.where(late, away["inner"], away["outer"])
        size_first = jnp.where(late, dims["inner"], dims["outer"])
        size_second = jnp.where(late, dims["outer"], dims["inner"])
        half = jnp.where(late, 1, 0)
        spot = ((away["core"] * 2 + half) * size_second + second) * size_first + first
        spot = spot * dims["line"] + away["line"]
        return spot * half_blocks + jnp.where(late, local - half_blocks, local)

    def block_copy(slot):
        at = lax.rem(slot, BUFFERS)
        return pltpu.make_async_copy(blocks_ref.at[slot], blocks_buf.at[at], block_sems.at[at])

    def start(slot):
        @pl.when(slot < count)
        def _():
            block_copy(slot).start()

    fills = []
    offset = 0
    for index, piece in enumerate(pieces):
        size = piece.shape[0]
        fills.append(
            pltpu.make_async_copy(
                piece, table_ref.at[pl.ds(offset, size)], piece_sems.at[index]
            )
        )
        offset += size
    for fill in fills:
        fill.start()
    for slot in range(AHEAD):
        start(slot)
    grad_ref[...] = jnp.zeros_like(grad_ref)
    for tile in range(tiles - LAG, tiles):
        pair_ref[tile] = jnp.zeros((width, rank), jnp.bfloat16)
        model_ref[tile] = jnp.zeros((edge, width), jnp.float32)
    total_ref[...] = jnp.zeros_like(total_ref)
    for fill in fills:
        fill.wait()

    def finish(tile, at, total):
        twice = blocks_buf[at, :, tile * width : (tile + 1) * width].astype(jnp.float32) * 2.0
        resid = ((jnp.tanh(model_ref[tile]) + 1.0) - twice).astype(jnp.bfloat16)
        return total + jnp.dot(resid, pair_ref[tile], preferred_element_type=jnp.float32)

    def step(slot, carry):
        start(slot + AHEAD)
        block_copy(slot).wait()
        at = lax.rem(slot, BUFFERS)
        before = jnp.maximum(slot - 1, 0)
        at_before = lax.rem(before, BUFFERS)
        place_b = row_place(1, slot)
        rows_a = table_ref[row_place(0, slot)] * jnp.asarray(0.5, jnp.bfloat16)
        rows_c = table_ref[row_place(2, slot)]
        total_before = total_ref[...]
        total = jnp.zeros((edge, rank), jnp.float32)
        for tile in range(tiles):
            if tile >= LAG:
                total = finish(tile - LAG, at, total)
            else:
                total_before = finish(tiles - LAG + tile, at_before, total_before)
            pair = jnp.concatenate(
                [
                    table_ref[place_b, pl.ds(tile * TILE_J + j, 1), :] * rows_c
                    for j in range(TILE_J)
                ],
                axis=0,
            )
            pair_ref[tile] = pair
            model_ref[tile] = lax.dot_general(
                rows_a, pair, (((1,), (1,)), ((), ())), preferred_element_type=jnp.float32
            )
        grad_ref[grad_place(before)] += 0.5 * total_before
        total_ref[...] = total
        return carry

    lax.fori_loop(0, count, step, 0)
    last = count - 1
    total = total_ref[...]
    for tile in range(tiles - LAG, tiles):
        total = finish(tile, lax.rem(last, BUFFERS), total)
    grad_ref[grad_place(last)] += 0.5 * total
    half = grad_ref.shape[0] // 2
    for index, out in enumerate((mine_ref, other_ref)):
        pltpu.make_async_copy(
            grad_ref.at[pl.ds(index * half, half)], out, out_sems.at[index]
        ).start()
    for index, out in enumerate((mine_ref, other_ref)):
        pltpu.make_async_copy(
            grad_ref.at[pl.ds(index * half, half)], out, out_sems.at[index]
        ).wait()


def per_device(tensor_blocks, block_coords, block_count, row_owner, factors, moment1, moment2):
    slot_count, edge, width = tensor_blocks.shape
    rank = factors.shape[2]
    local_blocks = moment1.shape[0] // edge
    row_blocks = row_owner.shape[1]
    dims = mesh_dims(lax.axis_size("blk"), lax.axis_size("grp"))
    shard = factors.astype(jnp.bfloat16).reshape(3 * local_blocks, edge, rank)
    halves = gather_rows(shard, dims)
    pieces = halves[0] + halves[1]
    smem = pl.BlockSpec(memory_space=pltpu.SMEM)
    hbm = pl.BlockSpec(memory_space=pl.ANY)
    tiles = edge // TILE_J
    outgoing = jax.ShapeDtypeStruct((row_blocks // 2, edge, rank), jnp.float32)
    mine, other = pl.pallas_call(
        functools.partial(slots_kernel, dims, local_blocks, len(pieces)),
        out_shape=(outgoing, outgoing),
        in_specs=[smem, smem, smem, hbm] + [hbm] * len(pieces),
        out_specs=(hbm, hbm),
        scratch_shapes=[
            pltpu.VMEM((3 * row_blocks, edge, rank), jnp.bfloat16),
            pltpu.VMEM((row_blocks, edge, rank), jnp.float32),
            pltpu.VMEM((BUFFERS, edge, width), jnp.bfloat16),
            pltpu.VMEM((tiles, TILE_J * edge, rank), jnp.bfloat16),
            pltpu.VMEM((tiles, edge, TILE_J * edge), jnp.float32),
            pltpu.VMEM((edge, rank), jnp.float32),
            pltpu.SemaphoreType.DMA((BUFFERS,)),
            pltpu.SemaphoreType.DMA((len(pieces),)),
            pltpu.SemaphoreType.DMA((2,)),
        ],
        compiler_params=pltpu.CompilerParams(vmem_limit_bytes=56 * 1024 * 1024),
        cost_estimate=pl.CostEstimate(
            flops=4 * slot_count * edge * width * rank,
            bytes_accessed=2 * slot_count * edge * width,
            transcendentals=slot_count * edge * width,
        ),
    )(block_coords, block_count, row_owner, tensor_blocks, *pieces)

    def by_half(values):
        values = values.reshape(2, row_blocks // 4, edge, rank)
        out = []
        for half, (first, second) in enumerate(ORDERS):
            out.append(
                values[half].reshape(
                    dims[second], dims[first], dims["line"], local_blocks // 2 * edge, rank
                )
            )
        return out

    arrived = by_half(shift(other, dims, "core", 1))
    kept_halves = by_half(mine)
    grads = []
    for half, (first, second) in enumerate(ORDERS):
        kept, got = kept_halves[half], [arrived[half]]
        for name in (second, first, "line"):
            sums = [
                functools.reduce(jnp.add, [g[k] for g in got], kept[k]) for k in range(dims[name])
            ]
            kept = sums[0]
            got = [shift(sums[k], dims, name, k) for k in range(1, dims[name])]
        grads.append(functools.reduce(jnp.add, got, kept))
    grad = jnp.concatenate(grads)
    new_moment1 = 0.9 * moment1 + 0.1 * grad
    new_moment2 = 0.999 * moment2 + 0.001 * grad * grad
    new_factor = factors[0] - 0.02 * (new_moment1 / (1.0 - 0.9**8)) / (
        jnp.sqrt(new_moment2 / (1.0 - 0.999**8)) + 1e-08
    )
    return (new_factor, new_moment1, new_moment2)


def solution(mesh):
    return jax.shard_map(
        per_device,
        mesh=mesh,
        in_specs=(
            P(AXES, None, None),
            P(None, AXES),
            P(AXES),
            P(),
            P(None, AXES, None),
            P(AXES, None),
            P(AXES, None),
        ),
        out_specs=(P(AXES, None), P(AXES, None), P(AXES, None)),
        check_vma=False,
    )
```

```python
import functools

import jax
import jax.numpy as jnp
from jax import lax
from jax.experimental import pallas as pl
from jax.experimental.pallas import tpu as pltpu
from jax.sharding import PartitionSpec as P

AXES = ("blk", "grp")
CORES = 2
BUFFERS = 4
AHEAD = 2
TILE_J = 4
QUARTERS = 4


def mesh_dims(blk, grp):
    chips = blk // CORES
    inner = 1
    for width in range(1, chips + 1):
        if chips % width == 0 and width * width <= chips:
            inner = width
    return {"outer": chips // inner, "inner": inner, "core": CORES, "line": grp}


def split_index(index, dims):
    line = lax.rem(index, dims["line"])
    rest = lax.div(index, dims["line"])
    core = lax.rem(rest, dims["core"])
    rest = lax.div(rest, dims["core"])
    return {
        "outer": lax.div(rest, dims["inner"]),
        "inner": lax.rem(rest, dims["inner"]),
        "core": core,
        "line": line,
    }


def shift(values, dims, name, step):
    strides = {
        "line": 1,
        "core": dims["line"],
        "inner": dims["line"] * dims["core"],
        "outer": dims["line"] * dims["core"] * dims["inner"],
    }
    total = strides["outer"] * dims["outer"]
    stride, size = strides[name], dims[name]
    perm = []
    for source in range(total):
        at = source // stride % size
        perm.append((source, source + ((at + step) % size - at) * stride))
    return lax.ppermute(values, AXES, perm)


ORDERS = (("outer", "inner"), ("inner", "outer"))
SIDE_ORDER = ("outer", "inner", "line")
SIDE_ROWS = 16


def gather_rows(shard, dims):
    cut = shard.shape[0] // 2
    side = shard[:, :SIDE_ROWS]
    main = shard[:, SIDE_ROWS:]
    line = [main] + [shift(main, dims, "line", k) for k in range(1, dims["line"])]
    for name in SIDE_ORDER[:2]:
        side = jnp.concatenate([side] + [shift(side, dims, name, k) for k in range(1, dims[name])])
    sides = [side] + [shift(side, dims, SIDE_ORDER[2], k) for k in range(1, dims[SIDE_ORDER[2]])]
    mains = []
    for part, (first, second) in zip((slice(0, cut), slice(cut, None)), ORDERS):
        own = jnp.concatenate([piece[part] for piece in line])
        own = jnp.concatenate([own] + [shift(own, dims, first, k) for k in range(1, dims[first])])
        mains.append([own] + [shift(own, dims, second, k) for k in range(1, dims[second])])
    mains = [pieces + [shift(piece, dims, "core", 1) for piece in pieces] for pieces in mains]
    sides = sides + [shift(piece, dims, "core", 1) for piece in sides]
    return mains[0] + mains[1], sides


def reduce_along(kept, got, dims, names):
    for name in names:
        sums = [functools.reduce(jnp.add, [g[k] for g in got], kept[k]) for k in range(dims[name])]
        kept = sums[0]
        got = [shift(sums[k], dims, name, k) for k in range(1, dims[name])]
    return functools.reduce(jnp.add, got, kept)


def away_from(there, here, dims):
    return {name: lax.rem(there[name] - here[name] + dims[name], dims[name]) for name in dims}


def main_spot(away, late, dims):
    second = jnp.where(late, away["outer"], away["inner"])
    first = jnp.where(late, away["inner"], away["outer"])
    size_first = jnp.where(late, dims["inner"], dims["outer"])
    size_second = jnp.where(late, dims["outer"], dims["inner"])
    return (second * size_first + first) * dims["line"] + away["line"], size_first * size_second


def side_spot(away, dims):
    spot = away["core"]
    for name in SIDE_ORDER[::-1]:
        spot = spot * dims[name] + away[name]
    return spot


def slots_kernel(dims, local_blocks, main_count, piece_count, *refs):
    coords_ref, count_ref, owner_ref, blocks_ref = refs[:4]
    pieces = refs[4 : 4 + piece_count]
    (
        mine_main_ref,
        other_main_ref,
        mine_side_ref,
        other_side_ref,
        main_ref,
        side_ref,
        grad_main_ref,
        grad_side_ref,
        blocks_buf,
        weight_ref,
        pair_ref,
        model_ref,
        total_ref,
        block_sems,
        piece_sems,
        out_sems,
    ) = refs[4 + piece_count :]
    edge, rank = total_ref.shape
    tiles = pair_ref.shape[0]
    width = TILE_J * edge
    quarter = edge * edge // QUARTERS
    count = count_ref[0]
    here = split_index(lax.axis_index("blk") * dims["line"] + lax.axis_index("grp"), dims)
    columns = dims["core"] * dims["outer"] * dims["inner"] * dims["line"]
    cut = 3 * local_blocks // 2
    half_blocks = local_blocks // 2

    def row_places(mode, slot):
        pos = owner_ref[mode, coords_ref[mode, slot]]
        there = split_index(lax.div(pos, local_blocks), dims)
        away = away_from(here, there, dims)
        block = mode * local_blocks + lax.rem(pos, local_blocks)
        late = block >= cut
        spot, size = main_spot(away, late, dims)
        spot = away["core"] * size * dims["line"] + spot
        blocks_of = jnp.where(late, 3 * local_blocks - cut, cut)
        main = jnp.where(late, columns * cut + block - cut, block) + spot * blocks_of
        side = side_spot(away, dims) * (3 * local_blocks) + block
        return main, side

    def grad_places(slot):
        pos = owner_ref[0, coords_ref[0, slot]]
        there = split_index(lax.div(pos, local_blocks), dims)
        away = away_from(there, here, dims)
        local = lax.rem(pos, local_blocks)
        late = local >= half_blocks
        spot, size = main_spot(away, late, dims)
        half = jnp.where(late, 1, 0)
        spot = (away["core"] * 2 + half) * size * dims["line"] + spot
        main = spot * half_blocks + jnp.where(late, local - half_blocks, local)
        side = side_spot(away, dims) * local_blocks + local
        return main, side

    def rows_of(places):
        main, side = places
        return jnp.concatenate([side_ref[side], main_ref[main]], axis=0)

    def row_of(places, j):
        main, side = places
        if j < SIDE_ROWS:
            return side_ref[side, pl.ds(j, 1), :]
        return main_ref[main, pl.ds(j - SIDE_ROWS, 1), :]

    def block_copy(slot):
        at = lax.rem(slot, BUFFERS)
        return pltpu.make_async_copy(blocks_ref.at[slot], blocks_buf.at[at], block_sems.at[at])

    def start(slot):
        @pl.when(slot < count)
        def _():
            block_copy(slot).start()

    fills = []
    for table, group in ((main_ref, range(main_count)), (side_ref, range(main_count, piece_count))):
        offset = 0
        for index in group:
            size = pieces[index].shape[0]
            fills.append(
                pltpu.make_async_copy(
                    pieces[index], table.at[pl.ds(offset, size)], piece_sems.at[index]
                )
            )
            offset += size
    for fill in fills:
        fill.start()
    for slot in range(AHEAD):
        start(slot)
    grad_main_ref[...] = jnp.zeros_like(grad_main_ref)
    grad_side_ref[...] = jnp.zeros_like(grad_side_ref)
    weight_ref[...] = jnp.zeros_like(weight_ref)
    pair_ref[tiles - 1] = jnp.zeros(pair_ref.shape[1:], pair_ref.dtype)
    model_ref[tiles - 1] = jnp.zeros(model_ref.shape[1:], model_ref.dtype)
    total_ref[...] = jnp.zeros_like(total_ref)
    for fill in fills:
        fill.wait()

    def finish(tile, at, total):
        model = model_ref[tile].T
        for q in range(QUARTERS):
            begin = q * quarter + tile * width
            twice = blocks_buf[at, :, begin : begin + width].astype(jnp.float32) * 2.0
            resid = ((jnp.tanh(model[q * edge : (q + 1) * edge]) + 1.0) - twice).astype(jnp.bfloat16)
            total = total + jnp.dot(
                resid,
                pair_ref[tile, :, q * rank : (q + 1) * rank],
                preferred_element_type=jnp.float32,
            )
        return total

    def add_total(slot, total):
        main, side = grad_places(slot)
        half = 0.5 * total
        grad_side_ref[side] += half[:SIDE_ROWS]
        grad_main_ref[main] += half[SIDE_ROWS:]

    lanes = lax.broadcasted_iota(jnp.int32, (rank, 2 * edge), 1)

    def step(slot, carry):
        start(slot + AHEAD)
        block_copy(slot).wait()
        at = lax.rem(slot, BUFFERS)
        before = jnp.maximum(slot - 1, 0)
        at_before = lax.rem(before, BUFFERS)
        places_b = row_places(1, slot)
        rows_a = rows_of(row_places(0, slot)).astype(jnp.float32) * 0.5
        twice_a = jnp.concatenate([rows_a, rows_a], axis=0).T
        for q in range(QUARTERS):
            keep = (lanes < edge) if q % 2 == 0 else (lanes >= edge)
            lane = q // 2 * 2 * edge
            weight_ref[q * rank : (q + 1) * rank, lane : lane + 2 * edge] = jnp.where(
                keep, twice_a, 0.0
            ).astype(jnp.bfloat16)
        rows_c = rows_of(row_places(2, slot))
        total_before = total_ref[...]
        total = jnp.zeros((edge, rank), jnp.float32)
        for tile in range(tiles):
            for q in range(QUARTERS):
                for j in range(TILE_J):
                    row = row_of(places_b, q * (edge // QUARTERS) + tile * TILE_J + j)
                    pair_ref[tile, j * edge : (j + 1) * edge, q * rank : (q + 1) * rank] = (
                        row * rows_c
                    )
            model_ref[tile] = jnp.dot(
                pair_ref[tile], weight_ref[...], preferred_element_type=jnp.float32
            )
            if tile == 0:
                total_before = finish(tiles - 1, at_before, total_before)
            else:
                total = finish(tile - 1, at, total)
        add_total(before, total_before)
        total_ref[...] = total
        return carry

    lax.fori_loop(0, count, step, 0)
    last = count - 1
    add_total(last, finish(tiles - 1, lax.rem(last, BUFFERS), total_ref[...]))
    drains = []
    for index, (grad, out, part) in enumerate(
        (
            (grad_main_ref, other_main_ref, 1),
            (grad_side_ref, other_side_ref, 1),
            (grad_main_ref, mine_main_ref, 0),
            (grad_side_ref, mine_side_ref, 0),
        )
    ):
        half = out.shape[0]
        drains.append(
            pltpu.make_async_copy(grad.at[pl.ds(part * half, half)], out, out_sems.at[index])
        )
    for drain in drains:
        drain.start()
    for drain in drains:
        drain.wait()


def per_device(tensor_blocks, block_coords, block_count, row_owner, factors, moment1, moment2):
    slot_count, edge, width = tensor_blocks.shape
    rank = factors.shape[2]
    local_blocks = moment1.shape[0] // edge
    row_blocks = row_owner.shape[1]
    dims = mesh_dims(lax.axis_size("blk"), lax.axis_size("grp"))
    shard = factors.astype(jnp.bfloat16).reshape(3 * local_blocks, edge, rank)
    mains, sides = gather_rows(shard, dims)
    pieces = mains + sides
    smem = pl.BlockSpec(memory_space=pltpu.SMEM)
    hbm = pl.BlockSpec(memory_space=pl.ANY)
    tiles = edge // (QUARTERS * TILE_J)
    main_rows = edge - SIDE_ROWS
    out_main = jax.ShapeDtypeStruct((row_blocks // 2, main_rows, rank), jnp.float32)
    out_side = jax.ShapeDtypeStruct((row_blocks // 2, SIDE_ROWS, rank), jnp.float32)
    mine_main, other_main, mine_side, other_side = pl.pallas_call(
        functools.partial(slots_kernel, dims, local_blocks, len(mains), len(pieces)),
        out_shape=(out_main, out_main, out_side, out_side),
        in_specs=[smem, smem, smem, hbm] + [hbm] * len(pieces),
        out_specs=(hbm, hbm, hbm, hbm),
        scratch_shapes=[
            pltpu.VMEM((3 * row_blocks, main_rows, rank), jnp.bfloat16),
            pltpu.VMEM((3 * row_blocks, SIDE_ROWS, rank), jnp.bfloat16),
            pltpu.VMEM((row_blocks, main_rows, rank), jnp.float32),
            pltpu.VMEM((row_blocks, SIDE_ROWS, rank), jnp.float32),
            pltpu.VMEM((BUFFERS, edge, width), jnp.bfloat16),
            pltpu.VMEM((QUARTERS * rank, QUARTERS * edge), jnp.bfloat16),
            pltpu.VMEM((tiles, TILE_J * edge, QUARTERS * rank), jnp.bfloat16),
            pltpu.VMEM((tiles, TILE_J * edge, QUARTERS * edge), jnp.float32),
            pltpu.VMEM((edge, rank), jnp.float32),
            pltpu.SemaphoreType.DMA((BUFFERS,)),
            pltpu.SemaphoreType.DMA((len(pieces),)),
            pltpu.SemaphoreType.DMA((4,)),
        ],
        compiler_params=pltpu.CompilerParams(vmem_limit_bytes=56 * 1024 * 1024),
        cost_estimate=pl.CostEstimate(
            flops=4 * slot_count * edge * width * rank,
            bytes_accessed=2 * slot_count * edge * width,
            transcendentals=slot_count * edge * width,
        ),
    )(block_coords, block_count, row_owner, tensor_blocks, *pieces)
    arrived_main = shift(other_main, dims, "core", 1)
    arrived_side = shift(other_side, dims, "core", 1)
    side_shape = tuple(dims[name] for name in SIDE_ORDER[::-1]) + (local_blocks, SIDE_ROWS, rank)
    side_grad = reduce_along(
        mine_side.reshape(side_shape), [arrived_side.reshape(side_shape)], dims, SIDE_ORDER[::-1]
    )
    main_grads = []
    for half, (first, second) in enumerate(ORDERS):
        shape = (2, dims[second], dims[first], dims["line"], local_blocks // 2, main_rows, rank)
        main_grads.append(
            reduce_along(
                mine_main.reshape(shape)[half],
                [arrived_main.reshape(shape)[half]],
                dims,
                (second, first, "line"),
            )
        )
    grad = jnp.concatenate([side_grad, jnp.concatenate(main_grads)], axis=1)
    grad = grad.reshape(local_blocks * edge, rank)
    new_moment1 = 0.9 * moment1 + 0.1 * grad
    new_moment2 = 0.999 * moment2 + 0.001 * grad * grad
    new_factor = factors[0] - 0.02 * (new_moment1 / (1.0 - 0.9**8)) / (
        jnp.sqrt(new_moment2 / (1.0 - 0.999**8)) + 1e-08
    )
    return (new_factor, new_moment1, new_moment2)


def solution(mesh):
    return jax.shard_map(
        per_device,
        mesh=mesh,
        in_specs=(
            P(AXES, None, None),
            P(None, AXES),
            P(AXES),
            P(),
            P(None, AXES, None),
            P(AXES, None),
            P(AXES, None),
        ),
        out_specs=(P(AXES, None), P(AXES, None), P(AXES, None)),
        check_vma=False,
    )
```

```python
import functools

import jax
import jax.numpy as jnp
from jax import lax
from jax.experimental import pallas as pl
from jax.experimental.pallas import tpu as pltpu
from jax.sharding import PartitionSpec as P

AXES = ("blk", "grp")
CORES = 2
BUFFERS = 5
AHEAD = 3
COPY_PARTS = 4
TILE_J = 16
LAG = 1


def mesh_dims(blk, grp):
    chips = blk // CORES
    inner = 1
    for width in range(1, chips + 1):
        if chips % width == 0 and width * width <= chips:
            inner = width
    return {"outer": chips // inner, "inner": inner, "core": CORES, "line": grp}


def split_index(index, dims):
    line = lax.rem(index, dims["line"])
    rest = lax.div(index, dims["line"])
    core = lax.rem(rest, dims["core"])
    rest = lax.div(rest, dims["core"])
    return {
        "outer": lax.div(rest, dims["inner"]),
        "inner": lax.rem(rest, dims["inner"]),
        "core": core,
        "line": line,
    }


def shift(values, dims, name, step):
    strides = {
        "line": 1,
        "core": dims["line"],
        "inner": dims["line"] * dims["core"],
        "outer": dims["line"] * dims["core"] * dims["inner"],
    }
    total = strides["outer"] * dims["outer"]
    stride, size = strides[name], dims[name]
    perm = []
    for source in range(total):
        at = source // stride % size
        perm.append((source, source + ((at + step) % size - at) * stride))
    return lax.ppermute(values, AXES, perm)


ORDERS = (("outer", "inner"), ("inner", "outer"))


def gather_rows(shard, dims):
    count = shard.shape[0]
    cut = count // 2
    line = [shard] + [shift(shard, dims, "line", k) for k in range(1, dims["line"])]
    halves = []
    for part, (first, second) in zip((slice(0, cut), slice(cut, count)), ORDERS):
        own = jnp.concatenate([piece[part] for piece in line])
        own = jnp.concatenate([own] + [shift(own, dims, first, k) for k in range(1, dims[first])])
        pieces = [own] + [shift(own, dims, second, k) for k in range(1, dims[second])]
        pieces = pieces + [shift(piece, dims, "core", 1) for piece in pieces]
        halves.append(pieces)
    return halves


def slots_kernel(dims, local_blocks, piece_count, *refs):
    coords_ref, count_ref, owner_ref, blocks_ref = refs[:4]
    pieces = refs[4 : 4 + piece_count]
    (
        mine_ref,
        other_ref,
        table_ref,
        grad_ref,
        blocks_buf,
        pair_ref,
        model_ref,
        total_ref,
        block_sems,
        piece_sems,
        out_sems,
    ) = refs[4 + piece_count :]
    edge, rank = grad_ref.shape[1], grad_ref.shape[2]
    width = TILE_J * edge
    tiles = edge // TILE_J
    count = count_ref[0]
    cut = 3 * local_blocks // 2
    here = split_index(lax.axis_index("blk") * dims["line"] + lax.axis_index("grp"), dims)
    columns = dims["core"] * dims["outer"] * dims["inner"] * dims["line"]

    def row_place(mode, slot):
        pos = owner_ref[mode, coords_ref[mode, slot]]
        there = split_index(lax.div(pos, local_blocks), dims)
        away = {
            name: lax.rem(here[name] - there[name] + dims[name], dims[name]) for name in dims
        }
        block = mode * local_blocks + lax.rem(pos, local_blocks)
        late = block >= cut
        second = jnp.where(late, away["outer"], away["inner"])
        first = jnp.where(late, away["inner"], away["outer"])
        size_first = jnp.where(late, dims["inner"], dims["outer"])
        size_second = jnp.where(late, dims["outer"], dims["inner"])
        spot = ((away["core"] * size_second + second) * size_first + first) * dims["line"]
        spot = spot + away["line"]
        blocks_of = jnp.where(late, 3 * local_blocks - cut, cut)
        base = jnp.where(late, columns * cut, 0)
        return base + spot * blocks_of + jnp.where(late, block - cut, block)

    def grad_place(slot):
        pos = owner_ref[0, coords_ref[0, slot]]
        there = split_index(lax.div(pos, local_blocks), dims)
        away = {
            name: lax.rem(there[name] - here[name] + dims[name], dims[name]) for name in dims
        }
        local = lax.rem(pos, local_blocks)
        half_blocks = local_blocks // 2
        late = local >= half_blocks
        second = jnp.where(late, away["outer"], away["inner"])
        first = jnp.where(late, away["inner"], away["outer"])
        size_first = jnp.where(late, dims["inner"], dims["outer"])
        size_second = jnp.where(late, dims["outer"], dims["inner"])
        half = jnp.where(late, 1, 0)
        spot = ((away["core"] * 2 + half) * size_second + second) * size_first + first
        spot = spot * dims["line"] + away["line"]
        return spot * half_blocks + jnp.where(late, local - half_blocks, local)

    def block_copies(slot):
        at = lax.rem(slot, BUFFERS)
        span = edge // COPY_PARTS
        return [
            pltpu.make_async_copy(
                blocks_ref.at[slot, pl.ds(part * span, span)],
                blocks_buf.at[at, pl.ds(part * span, span)],
                block_sems.at[at, part],
            )
            for part in range(COPY_PARTS)
        ]

    def start(slot):
        @pl.when(slot < count)
        def _():
            for copy in block_copies(slot):
                copy.start()

    fills = []
    offset = 0
    for index, piece in enumerate(pieces):
        size = piece.shape[0]
        fills.append(
            pltpu.make_async_copy(
                piece, table_ref.at[pl.ds(offset, size)], piece_sems.at[index]
            )
        )
        offset += size
    for fill in fills:
        fill.start()
    for slot in range(AHEAD):
        start(slot)
    grad_ref[...] = jnp.zeros_like(grad_ref)
    for tile in range(tiles - LAG, tiles):
        pair_ref[tile] = jnp.zeros((width, rank), jnp.bfloat16)
        model_ref[tile] = jnp.zeros((edge, width), jnp.float32)
    total_ref[...] = jnp.zeros_like(total_ref)
    for fill in fills:
        fill.wait()

    def finish(tile, at, total):
        twice = blocks_buf[at, :, tile * width : (tile + 1) * width].astype(jnp.float32) * 2.0
        resid = ((jnp.tanh(model_ref[tile]) + 1.0) - twice).astype(jnp.bfloat16)
        return total + jnp.dot(resid, pair_ref[tile], preferred_element_type=jnp.float32)

    def step(slot, carry):
        start(slot + AHEAD)
        for copy in block_copies(slot):
            copy.wait()
        at = lax.rem(slot, BUFFERS)
        before = jnp.maximum(slot - 1, 0)
        at_before = lax.rem(before, BUFFERS)
        place_b = row_place(1, slot)
        rows_a = table_ref[row_place(0, slot)] * jnp.asarray(0.5, jnp.bfloat16)
        rows_c = table_ref[row_place(2, slot)]
        total_before = total_ref[...]
        total = jnp.zeros((edge, rank), jnp.float32)
        for tile in range(tiles):
            if tile >= LAG:
                total = finish(tile - LAG, at, total)
            else:
                total_before = finish(tiles - LAG + tile, at_before, total_before)
            pair = jnp.concatenate(
                [
                    table_ref[place_b, pl.ds(tile * TILE_J + j, 1), :] * rows_c
                    for j in range(TILE_J)
                ],
                axis=0,
            )
            pair_ref[tile] = pair
            model_ref[tile] = lax.dot_general(
                rows_a, pair, (((1,), (1,)), ((), ())), preferred_element_type=jnp.float32
            )
        grad_ref[grad_place(before)] += 0.5 * total_before
        total_ref[...] = total
        return carry

    lax.fori_loop(0, count, step, 0)
    last = count - 1
    total = total_ref[...]
    for tile in range(tiles - LAG, tiles):
        total = finish(tile, lax.rem(last, BUFFERS), total)
    grad_ref[grad_place(last)] += 0.5 * total
    half = grad_ref.shape[0] // 2
    for index, out in enumerate((mine_ref, other_ref)):
        pltpu.make_async_copy(
            grad_ref.at[pl.ds(index * half, half)], out, out_sems.at[index]
        ).start()
    for index, out in enumerate((mine_ref, other_ref)):
        pltpu.make_async_copy(
            grad_ref.at[pl.ds(index * half, half)], out, out_sems.at[index]
        ).wait()


def per_device(tensor_blocks, block_coords, block_count, row_owner, factors, moment1, moment2):
    slot_count, edge, width = tensor_blocks.shape
    rank = factors.shape[2]
    local_blocks = moment1.shape[0] // edge
    row_blocks = row_owner.shape[1]
    dims = mesh_dims(lax.axis_size("blk"), lax.axis_size("grp"))
    shard = factors.astype(jnp.bfloat16).reshape(3 * local_blocks, edge, rank)
    halves = gather_rows(shard, dims)
    pieces = halves[0] + halves[1]
    smem = pl.BlockSpec(memory_space=pltpu.SMEM)
    hbm = pl.BlockSpec(memory_space=pl.ANY)
    tiles = edge // TILE_J
    outgoing = jax.ShapeDtypeStruct((row_blocks // 2, edge, rank), jnp.float32)
    mine, other = pl.pallas_call(
        functools.partial(slots_kernel, dims, local_blocks, len(pieces)),
        out_shape=(outgoing, outgoing),
        in_specs=[smem, smem, smem, hbm] + [hbm] * len(pieces),
        out_specs=(hbm, hbm),
        scratch_shapes=[
            pltpu.VMEM((3 * row_blocks, edge, rank), jnp.bfloat16),
            pltpu.VMEM((row_blocks, edge, rank), jnp.float32),
            pltpu.VMEM((BUFFERS, edge, width), jnp.bfloat16),
            pltpu.VMEM((tiles, TILE_J * edge, rank), jnp.bfloat16),
            pltpu.VMEM((tiles, edge, TILE_J * edge), jnp.float32),
            pltpu.VMEM((edge, rank), jnp.float32),
            pltpu.SemaphoreType.DMA((BUFFERS, COPY_PARTS)),
            pltpu.SemaphoreType.DMA((len(pieces),)),
            pltpu.SemaphoreType.DMA((2,)),
        ],
        compiler_params=pltpu.CompilerParams(vmem_limit_bytes=56 * 1024 * 1024),
        cost_estimate=pl.CostEstimate(
            flops=4 * slot_count * edge * width * rank,
            bytes_accessed=2 * slot_count * edge * width,
            transcendentals=slot_count * edge * width,
        ),
    )(block_coords, block_count, row_owner, tensor_blocks, *pieces)

    def by_half(values):
        values = values.reshape(2, row_blocks // 4, edge, rank)
        out = []
        for half, (first, second) in enumerate(ORDERS):
            out.append(
                values[half].reshape(
                    dims[second], dims[first], dims["line"], local_blocks // 2 * edge, rank
                )
            )
        return out

    arrived = by_half(shift(other, dims, "core", 1))
    kept_halves = by_half(mine)
    sums = []
    for half, (first, second) in enumerate(ORDERS):
        kept, got = kept_halves[half], [arrived[half]]
        for name in (second, first):
            terms = [
                functools.reduce(jnp.add, [g[k] for g in got], kept[k]) for k in range(dims[name])
            ]
            kept = terms[0]
            got = [shift(terms[k], dims, name, k) for k in range(1, dims[name])]
        sums.append(functools.reduce(jnp.add, got, kept))
    rows = [jnp.concatenate([part[k] for part in sums]) for k in range(dims["line"])]
    grad = rows[0]
    for k in range(1, dims["line"]):
        grad = grad + shift(rows[k], dims, "line", k)
    new_moment1 = 0.9 * moment1 + 0.1 * grad
    new_moment2 = 0.999 * moment2 + 0.001 * grad * grad
    new_factor = factors[0] - 0.02 * (new_moment1 / (1.0 - 0.9**8)) / (
        jnp.sqrt(new_moment2 / (1.0 - 0.999**8)) + 1e-08
    )
    return (new_factor, new_moment1, new_moment2)


def solution(mesh):
    return jax.shard_map(
        per_device,
        mesh=mesh,
        in_specs=(
            P(AXES, None, None),
            P(None, AXES),
            P(AXES),
            P(),
            P(None, AXES, None),
            P(AXES, None),
            P(AXES, None),
        ),
        out_specs=(P(AXES, None), P(AXES, None), P(AXES, None)),
        check_vma=False,
    )
```

```python
import functools

import jax
import jax.numpy as jnp
from jax import lax
from jax.experimental import pallas as pl
from jax.experimental.pallas import tpu as pltpu
from jax.sharding import PartitionSpec as P

AXES = ("blk", "grp")
CORES = 2
BUFFERS = 5
AHEAD = 3
COPY_PARTS = 4
TILE_J = 32
SIDE_ROWS = 16
LAG = 1


def mesh_dims(blk, grp):
    chips = blk // CORES
    inner = 1
    for width in range(1, chips + 1):
        if chips % width == 0 and width * width <= chips:
            inner = width
    return {"outer": chips // inner, "inner": inner, "core": CORES, "line": grp}


def split_index(index, dims):
    line = lax.rem(index, dims["line"])
    rest = lax.div(index, dims["line"])
    core = lax.rem(rest, dims["core"])
    rest = lax.div(rest, dims["core"])
    return {
        "outer": lax.div(rest, dims["inner"]),
        "inner": lax.rem(rest, dims["inner"]),
        "core": core,
        "line": line,
    }


def shift(values, dims, name, step):
    strides = {
        "line": 1,
        "core": dims["line"],
        "inner": dims["line"] * dims["core"],
        "outer": dims["line"] * dims["core"] * dims["inner"],
    }
    total = strides["outer"] * dims["outer"]
    stride, size = strides[name], dims[name]
    perm = []
    for source in range(total):
        at = source // stride % size
        perm.append((source, source + ((at + step) % size - at) * stride))
    return lax.ppermute(values, AXES, perm)


ORDERS = (("outer", "inner"), ("inner", "outer"))


def gather_rows(shard, dims):
    cut = shard.shape[0] // 2
    side = lax.all_gather(shard[:, :SIDE_ROWS], AXES, axis=0, tiled=True)
    main = shard[:, SIDE_ROWS:]
    line = [main] + [shift(main, dims, "line", k) for k in range(1, dims["line"])]
    mains = []
    for part, (first, second) in zip((slice(0, cut), slice(cut, None)), ORDERS):
        own = jnp.concatenate([piece[part] for piece in line])
        own = jnp.concatenate([own] + [shift(own, dims, first, k) for k in range(1, dims[first])])
        mains.append([own] + [shift(own, dims, second, k) for k in range(1, dims[second])])
    mains = [pieces + [shift(piece, dims, "core", 1) for piece in pieces] for pieces in mains]
    return mains[0] + mains[1], [side]


def slots_kernel(dims, local_blocks, main_count, piece_count, *refs):
    coords_ref, count_ref, owner_ref, blocks_ref = refs[:4]
    pieces = refs[4 : 4 + piece_count]
    (
        mine_ref,
        other_ref,
        main_ref,
        side_ref,
        grad_ref,
        blocks_buf,
        pair_ref,
        model_ref,
        total_ref,
        block_sems,
        piece_sems,
        out_sems,
    ) = refs[4 + piece_count :]
    edge, rank = grad_ref.shape[1], grad_ref.shape[2]
    width = TILE_J * edge
    tiles = edge // TILE_J
    count = count_ref[0]
    cut = 3 * local_blocks // 2
    here = split_index(lax.axis_index("blk") * dims["line"] + lax.axis_index("grp"), dims)
    columns = dims["core"] * dims["outer"] * dims["inner"] * dims["line"]

    def row_places(mode, slot):
        pos = owner_ref[mode, coords_ref[mode, slot]]
        there = split_index(lax.div(pos, local_blocks), dims)
        away = {
            name: lax.rem(here[name] - there[name] + dims[name], dims[name]) for name in dims
        }
        block = mode * local_blocks + lax.rem(pos, local_blocks)
        late = block >= cut
        second = jnp.where(late, away["outer"], away["inner"])
        first = jnp.where(late, away["inner"], away["outer"])
        size_first = jnp.where(late, dims["inner"], dims["outer"])
        size_second = jnp.where(late, dims["outer"], dims["inner"])
        spot = ((away["core"] * size_second + second) * size_first + first) * dims["line"]
        spot = spot + away["line"]
        blocks_of = jnp.where(late, 3 * local_blocks - cut, cut)
        main = jnp.where(late, columns * cut + block - cut, block) + spot * blocks_of
        side = lax.div(pos, local_blocks) * (3 * local_blocks) + block
        return main, side

    def rows_of(places):
        main, side = places
        return jnp.concatenate([side_ref[side], main_ref[main]], axis=0)

    def row_of(places, j):
        main, side = places
        if j < SIDE_ROWS:
            return side_ref[side, pl.ds(j, 1), :]
        return main_ref[main, pl.ds(j - SIDE_ROWS, 1), :]

    def grad_place(slot):
        pos = owner_ref[0, coords_ref[0, slot]]
        there = split_index(lax.div(pos, local_blocks), dims)
        away = {
            name: lax.rem(there[name] - here[name] + dims[name], dims[name]) for name in dims
        }
        local = lax.rem(pos, local_blocks)
        half_blocks = local_blocks // 2
        late = local >= half_blocks
        second = jnp.where(late, away["outer"], away["inner"])
        first = jnp.where(late, away["inner"], away["outer"])
        size_first = jnp.where(late, dims["inner"], dims["outer"])
        size_second = jnp.where(late, dims["outer"], dims["inner"])
        half = jnp.where(late, 1, 0)
        spot = ((away["core"] * 2 + half) * size_second + second) * size_first + first
        spot = spot * dims["line"] + away["line"]
        return spot * half_blocks + jnp.where(late, local - half_blocks, local)

    def block_copies(slot):
        at = lax.rem(slot, BUFFERS)
        span = edge // COPY_PARTS
        return [
            pltpu.make_async_copy(
                blocks_ref.at[slot, pl.ds(part * span, span)],
                blocks_buf.at[at, pl.ds(part * span, span)],
                block_sems.at[at, part],
            )
            for part in range(COPY_PARTS)
        ]

    def start(slot):
        @pl.when(slot < count)
        def _():
            for copy in block_copies(slot):
                copy.start()

    fills = []
    for table, group in ((main_ref, range(main_count)), (side_ref, range(main_count, piece_count))):
        offset = 0
        for index in group:
            size = pieces[index].shape[0]
            fills.append(
                pltpu.make_async_copy(
                    pieces[index], table.at[pl.ds(offset, size)], piece_sems.at[index]
                )
            )
            offset += size
    for fill in fills:
        fill.start()
    for slot in range(AHEAD):
        start(slot)
    grad_ref[...] = jnp.zeros_like(grad_ref)
    for tile in range(tiles - LAG, tiles):
        pair_ref[tile] = jnp.zeros((width, rank), jnp.bfloat16)
        model_ref[tile] = jnp.zeros((edge, width), jnp.float32)
    total_ref[...] = jnp.zeros_like(total_ref)
    for fill in fills:
        fill.wait()

    def finish(tile, at, total):
        twice = blocks_buf[at, :, tile * width : (tile + 1) * width].astype(jnp.float32) * 2.0
        resid = ((jnp.tanh(model_ref[tile]) + 1.0) - twice).astype(jnp.bfloat16)
        middle = width // 2
        low = jnp.dot(resid[:, :middle], pair_ref[tile, :middle], preferred_element_type=jnp.float32)
        high = jnp.dot(resid[:, middle:], pair_ref[tile, middle:], preferred_element_type=jnp.float32)
        return total + (low + high)

    def step(slot, carry):
        start(slot + AHEAD)
        for copy in block_copies(slot):
            copy.wait()
        at = lax.rem(slot, BUFFERS)
        before = jnp.maximum(slot - 1, 0)
        at_before = lax.rem(before, BUFFERS)
        places_b = row_places(1, slot)
        rows_a = rows_of(row_places(0, slot)) * jnp.asarray(0.5, jnp.bfloat16)
        rows_c = rows_of(row_places(2, slot))
        total_before = total_ref[...]
        total = jnp.zeros((edge, rank), jnp.float32)
        for tile in range(tiles):
            if tile >= LAG:
                total = finish(tile - LAG, at, total)
            else:
                total_before = finish(tiles - LAG + tile, at_before, total_before)
            pair = jnp.concatenate(
                [
                    row_of(places_b, tile * TILE_J + j) * rows_c
                    for j in range(TILE_J)
                ],
                axis=0,
            )
            pair_ref[tile] = pair
            model_ref[tile] = lax.dot_general(
                rows_a, pair, (((1,), (1,)), ((), ())), preferred_element_type=jnp.float32
            )
        grad_ref[grad_place(before)] += 0.5 * total_before
        total_ref[...] = total
        return carry

    lax.fori_loop(0, count, step, 0)
    last = count - 1
    total = total_ref[...]
    for tile in range(tiles - LAG, tiles):
        total = finish(tile, lax.rem(last, BUFFERS), total)
    grad_ref[grad_place(last)] += 0.5 * total
    half = grad_ref.shape[0] // 2
    for index, out in enumerate((mine_ref, other_ref)):
        pltpu.make_async_copy(
            grad_ref.at[pl.ds(index * half, half)], out, out_sems.at[index]
        ).start()
    for index, out in enumerate((mine_ref, other_ref)):
        pltpu.make_async_copy(
            grad_ref.at[pl.ds(index * half, half)], out, out_sems.at[index]
        ).wait()


def per_device(tensor_blocks, block_coords, block_count, row_owner, factors, moment1, moment2):
    slot_count, edge, width = tensor_blocks.shape
    rank = factors.shape[2]
    local_blocks = moment1.shape[0] // edge
    row_blocks = row_owner.shape[1]
    dims = mesh_dims(lax.axis_size("blk"), lax.axis_size("grp"))
    shard = factors.astype(jnp.bfloat16).reshape(3 * local_blocks, edge, rank)
    mains, sides = gather_rows(shard, dims)
    pieces = mains + sides
    smem = pl.BlockSpec(memory_space=pltpu.SMEM)
    hbm = pl.BlockSpec(memory_space=pl.ANY)
    tiles = edge // TILE_J
    outgoing = jax.ShapeDtypeStruct((row_blocks // 2, edge, rank), jnp.float32)
    mine, other = pl.pallas_call(
        functools.partial(slots_kernel, dims, local_blocks, len(mains), len(pieces)),
        out_shape=(outgoing, outgoing),
        in_specs=[smem, smem, smem, hbm] + [hbm] * len(pieces),
        out_specs=(hbm, hbm),
        scratch_shapes=[
            pltpu.VMEM((3 * row_blocks, edge - SIDE_ROWS, rank), jnp.bfloat16),
            pltpu.VMEM((3 * row_blocks, SIDE_ROWS, rank), jnp.bfloat16),
            pltpu.VMEM((row_blocks, edge, rank), jnp.float32),
            pltpu.VMEM((BUFFERS, edge, width), jnp.bfloat16),
            pltpu.VMEM((tiles, TILE_J * edge, rank), jnp.bfloat16),
            pltpu.VMEM((tiles, edge, TILE_J * edge), jnp.float32),
            pltpu.VMEM((edge, rank), jnp.float32),
            pltpu.SemaphoreType.DMA((BUFFERS, COPY_PARTS)),
            pltpu.SemaphoreType.DMA((len(pieces),)),
            pltpu.SemaphoreType.DMA((2,)),
        ],
        compiler_params=pltpu.CompilerParams(vmem_limit_bytes=56 * 1024 * 1024),
        cost_estimate=pl.CostEstimate(
            flops=4 * slot_count * edge * width * rank,
            bytes_accessed=2 * slot_count * edge * width,
            transcendentals=slot_count * edge * width,
        ),
    )(block_coords, block_count, row_owner, tensor_blocks, *pieces)

    def by_half(values):
        values = values.reshape(2, row_blocks // 4, edge, rank)
        out = []
        for half, (first, second) in enumerate(ORDERS):
            out.append(
                values[half].reshape(
                    dims[second], dims[first], dims["line"], local_blocks // 2 * edge, rank
                )
            )
        return out

    arrived = by_half(shift(other, dims, "core", 1))
    kept_halves = by_half(mine)
    sums = []
    for half, (first, second) in enumerate(ORDERS):
        kept, got = kept_halves[half], [arrived[half]]
        for name in (second, first):
            terms = [
                functools.reduce(jnp.add, [g[k] for g in got], kept[k]) for k in range(dims[name])
            ]
            kept = terms[0]
            got = [shift(terms[k], dims, name, k) for k in range(1, dims[name])]
        sums.append(functools.reduce(jnp.add, got, kept))
    rows = [jnp.concatenate([part[k] for part in sums]) for k in range(dims["line"])]
    grad = rows[0]
    for k in range(1, dims["line"]):
        grad = grad + shift(rows[k], dims, "line", k)
    new_moment1 = 0.9 * moment1 + 0.1 * grad
    new_moment2 = 0.999 * moment2 + 0.001 * grad * grad
    new_factor = factors[0] - 0.02 * (new_moment1 / (1.0 - 0.9**8)) / (
        jnp.sqrt(new_moment2 / (1.0 - 0.999**8)) + 1e-08
    )
    return (new_factor, new_moment1, new_moment2)


def solution(mesh):
    return jax.shard_map(
        per_device,
        mesh=mesh,
        in_specs=(
            P(AXES, None, None),
            P(None, AXES),
            P(AXES),
            P(),
            P(None, AXES, None),
            P(AXES, None),
            P(AXES, None),
        ),
        out_specs=(P(AXES, None), P(AXES, None), P(AXES, None)),
        check_vma=False,
    )
```

```python
import functools

import jax
import jax.numpy as jnp
from jax import lax
from jax.experimental import pallas as pl
from jax.experimental.pallas import tpu as pltpu
from jax.sharding import PartitionSpec as P

AXES = ("blk", "grp")
CORES = 2
BUFFERS = 5
AHEAD = 3
COPY_PARTS = 4
TILE_J = 8
QUARTERS = 4


def mesh_dims(blk, grp):
    chips = blk // CORES
    inner = 1
    for width in range(1, chips + 1):
        if chips % width == 0 and width * width <= chips:
            inner = width
    return {"outer": chips // inner, "inner": inner, "core": CORES, "line": grp}


def split_index(index, dims):
    line = lax.rem(index, dims["line"])
    rest = lax.div(index, dims["line"])
    core = lax.rem(rest, dims["core"])
    rest = lax.div(rest, dims["core"])
    return {
        "outer": lax.div(rest, dims["inner"]),
        "inner": lax.rem(rest, dims["inner"]),
        "core": core,
        "line": line,
    }


def shift(values, dims, name, step):
    strides = {
        "line": 1,
        "core": dims["line"],
        "inner": dims["line"] * dims["core"],
        "outer": dims["line"] * dims["core"] * dims["inner"],
    }
    total = strides["outer"] * dims["outer"]
    stride, size = strides[name], dims[name]
    perm = []
    for source in range(total):
        at = source // stride % size
        perm.append((source, source + ((at + step) % size - at) * stride))
    return lax.ppermute(values, AXES, perm)


ORDERS = (("outer", "inner"), ("inner", "outer"))


def gather_rows(shard, dims):
    count = shard.shape[0]
    cut = count // 2
    line = [shard] + [shift(shard, dims, "line", k) for k in range(1, dims["line"])]
    halves = []
    for part, (first, second) in zip((slice(0, cut), slice(cut, count)), ORDERS):
        own = jnp.concatenate([piece[part] for piece in line])
        own = jnp.concatenate([own] + [shift(own, dims, first, k) for k in range(1, dims[first])])
        pieces = [own] + [shift(own, dims, second, k) for k in range(1, dims[second])]
        pieces = pieces + [shift(piece, dims, "core", 1) for piece in pieces]
        halves.append(pieces)
    return halves


def slots_kernel(dims, local_blocks, piece_count, *refs):
    coords_ref, count_ref, owner_ref, blocks_ref = refs[:4]
    pieces = refs[4 : 4 + piece_count]
    (
        mine_ref,
        other_ref,
        table_ref,
        grad_ref,
        blocks_buf,
        pair_ref,
        weight_ref,
        model_ref,
        total_ref,
        block_sems,
        piece_sems,
        out_sems,
    ) = refs[4 + piece_count :]
    edge, rank = grad_ref.shape[1], grad_ref.shape[2]
    width = TILE_J * edge
    tiles = edge // (QUARTERS * TILE_J)
    count = count_ref[0]
    cut = 3 * local_blocks // 2
    here = split_index(lax.axis_index("blk") * dims["line"] + lax.axis_index("grp"), dims)
    columns = dims["core"] * dims["outer"] * dims["inner"] * dims["line"]

    def row_place(mode, slot):
        pos = owner_ref[mode, coords_ref[mode, slot]]
        there = split_index(lax.div(pos, local_blocks), dims)
        away = {
            name: lax.rem(here[name] - there[name] + dims[name], dims[name]) for name in dims
        }
        block = mode * local_blocks + lax.rem(pos, local_blocks)
        late = block >= cut
        second = jnp.where(late, away["outer"], away["inner"])
        first = jnp.where(late, away["inner"], away["outer"])
        size_first = jnp.where(late, dims["inner"], dims["outer"])
        size_second = jnp.where(late, dims["outer"], dims["inner"])
        spot = ((away["core"] * size_second + second) * size_first + first) * dims["line"]
        spot = spot + away["line"]
        blocks_of = jnp.where(late, 3 * local_blocks - cut, cut)
        base = jnp.where(late, columns * cut, 0)
        return base + spot * blocks_of + jnp.where(late, block - cut, block)

    def grad_place(slot):
        pos = owner_ref[0, coords_ref[0, slot]]
        there = split_index(lax.div(pos, local_blocks), dims)
        away = {
            name: lax.rem(there[name] - here[name] + dims[name], dims[name]) for name in dims
        }
        local = lax.rem(pos, local_blocks)
        half_blocks = local_blocks // 2
        late = local >= half_blocks
        second = jnp.where(late, away["outer"], away["inner"])
        first = jnp.where(late, away["inner"], away["outer"])
        size_first = jnp.where(late, dims["inner"], dims["outer"])
        size_second = jnp.where(late, dims["outer"], dims["inner"])
        half = jnp.where(late, 1, 0)
        spot = ((away["core"] * 2 + half) * size_second + second) * size_first + first
        spot = spot * dims["line"] + away["line"]
        return spot * half_blocks + jnp.where(late, local - half_blocks, local)

    def block_copies(slot):
        at = lax.rem(slot, BUFFERS)
        span = edge // COPY_PARTS
        return [
            pltpu.make_async_copy(
                blocks_ref.at[slot, pl.ds(part * span, span)],
                blocks_buf.at[at, pl.ds(part * span, span)],
                block_sems.at[at, part],
            )
            for part in range(COPY_PARTS)
        ]

    def start(slot):
        @pl.when(slot < count)
        def _():
            for copy in block_copies(slot):
                copy.start()

    fills = []
    offset = 0
    for index, piece in enumerate(pieces):
        size = piece.shape[0]
        fills.append(
            pltpu.make_async_copy(
                piece, table_ref.at[pl.ds(offset, size)], piece_sems.at[index]
            )
        )
        offset += size
    for fill in fills:
        fill.start()
    for slot in range(AHEAD):
        start(slot)
    grad_ref[...] = jnp.zeros_like(grad_ref)
    pair_ref[tiles - 1] = jnp.zeros(pair_ref.shape[1:], pair_ref.dtype)
    model_ref[tiles - 1] = jnp.zeros(model_ref.shape[1:], model_ref.dtype)
    weight_ref[...] = jnp.zeros_like(weight_ref)
    total_ref[...] = jnp.zeros_like(total_ref)
    for fill in fills:
        fill.wait()

    quarter = edge * edge // QUARTERS
    lanes = lax.broadcasted_iota(jnp.int32, (rank, 2 * edge), 1)

    def finish(tile, at, total):
        model = model_ref[tile].T
        for q in range(QUARTERS):
            begin = q * quarter + tile * width
            twice = blocks_buf[at, :, begin : begin + width].astype(jnp.float32) * 2.0
            resid = ((jnp.tanh(model[q * edge : (q + 1) * edge]) + 1.0) - twice).astype(jnp.bfloat16)
            total = total + jnp.dot(
                resid,
                pair_ref[tile, :, q * rank : (q + 1) * rank],
                preferred_element_type=jnp.float32,
            )
        return total

    def step(slot, carry):
        start(slot + AHEAD)
        for copy in block_copies(slot):
            copy.wait()
        at = lax.rem(slot, BUFFERS)
        before = jnp.maximum(slot - 1, 0)
        at_before = lax.rem(before, BUFFERS)
        place_b = row_place(1, slot)
        rows_a = table_ref[row_place(0, slot)].astype(jnp.float32) * 0.5
        twice_a = jnp.concatenate([rows_a, rows_a], axis=0).T
        for q in range(QUARTERS):
            keep = (lanes < edge) if q % 2 == 0 else (lanes >= edge)
            lane = q // 2 * 2 * edge
            weight_ref[q * rank : (q + 1) * rank, lane : lane + 2 * edge] = jnp.where(
                keep, twice_a, 0.0
            ).astype(jnp.bfloat16)
        rows_c = table_ref[row_place(2, slot)]
        total_before = total_ref[...]
        total = jnp.zeros((edge, rank), jnp.float32)
        for tile in range(tiles):
            if tile == 0:
                total_before = finish(tiles - 1, at_before, total_before)
            else:
                total = finish(tile - 1, at, total)
            for q in range(QUARTERS):
                for j in range(TILE_J):
                    row = table_ref[
                        place_b, pl.ds(q * (edge // QUARTERS) + tile * TILE_J + j, 1), :
                    ]
                    pair_ref[tile, j * edge : (j + 1) * edge, q * rank : (q + 1) * rank] = (
                        row * rows_c
                    )
            model_ref[tile] = jnp.dot(
                pair_ref[tile], weight_ref[...], preferred_element_type=jnp.float32
            )
        grad_ref[grad_place(before)] += 0.5 * total_before
        total_ref[...] = total
        return carry

    lax.fori_loop(0, count, step, 0)
    last = count - 1
    grad_ref[grad_place(last)] += 0.5 * finish(tiles - 1, lax.rem(last, BUFFERS), total_ref[...])
    half = grad_ref.shape[0] // 2
    for index, out in enumerate((mine_ref, other_ref)):
        pltpu.make_async_copy(
            grad_ref.at[pl.ds(index * half, half)], out, out_sems.at[index]
        ).start()
    for index, out in enumerate((mine_ref, other_ref)):
        pltpu.make_async_copy(
            grad_ref.at[pl.ds(index * half, half)], out, out_sems.at[index]
        ).wait()


def per_device(tensor_blocks, block_coords, block_count, row_owner, factors, moment1, moment2):
    slot_count, edge, width = tensor_blocks.shape
    rank = factors.shape[2]
    local_blocks = moment1.shape[0] // edge
    row_blocks = row_owner.shape[1]
    dims = mesh_dims(lax.axis_size("blk"), lax.axis_size("grp"))
    shard = factors.astype(jnp.bfloat16).reshape(3 * local_blocks, edge, rank)
    halves = gather_rows(shard, dims)
    pieces = halves[0] + halves[1]
    smem = pl.BlockSpec(memory_space=pltpu.SMEM)
    hbm = pl.BlockSpec(memory_space=pl.ANY)
    tiles = edge // (QUARTERS * TILE_J)
    outgoing = jax.ShapeDtypeStruct((row_blocks // 2, edge, rank), jnp.float32)
    mine, other = pl.pallas_call(
        functools.partial(slots_kernel, dims, local_blocks, len(pieces)),
        out_shape=(outgoing, outgoing),
        in_specs=[smem, smem, smem, hbm] + [hbm] * len(pieces),
        out_specs=(hbm, hbm),
        scratch_shapes=[
            pltpu.VMEM((3 * row_blocks, edge, rank), jnp.bfloat16),
            pltpu.VMEM((row_blocks, edge, rank), jnp.float32),
            pltpu.VMEM((BUFFERS, edge, width), jnp.bfloat16),
            pltpu.VMEM((tiles, TILE_J * edge, QUARTERS * rank), jnp.bfloat16),
            pltpu.VMEM((QUARTERS * rank, QUARTERS * edge), jnp.bfloat16),
            pltpu.VMEM((tiles, TILE_J * edge, QUARTERS * edge), jnp.float32),
            pltpu.VMEM((edge, rank), jnp.float32),
            pltpu.SemaphoreType.DMA((BUFFERS, COPY_PARTS)),
            pltpu.SemaphoreType.DMA((len(pieces),)),
            pltpu.SemaphoreType.DMA((2,)),
        ],
        compiler_params=pltpu.CompilerParams(vmem_limit_bytes=56 * 1024 * 1024),
        cost_estimate=pl.CostEstimate(
            flops=4 * slot_count * edge * width * rank,
            bytes_accessed=2 * slot_count * edge * width,
            transcendentals=slot_count * edge * width,
        ),
    )(block_coords, block_count, row_owner, tensor_blocks, *pieces)

    def by_half(values):
        values = values.reshape(2, row_blocks // 4, edge, rank)
        out = []
        for half, (first, second) in enumerate(ORDERS):
            out.append(
                values[half].reshape(
                    dims[second], dims[first], dims["line"], local_blocks // 2 * edge, rank
                )
            )
        return out

    arrived = by_half(shift(other, dims, "core", 1))
    kept_halves = by_half(mine)
    sums = []
    for half, (first, second) in enumerate(ORDERS):
        kept, got = kept_halves[half], [arrived[half]]
        for name in (second, first):
            terms = [
                functools.reduce(jnp.add, [g[k] for g in got], kept[k]) for k in range(dims[name])
            ]
            kept = terms[0]
            got = [shift(terms[k], dims, name, k) for k in range(1, dims[name])]
        sums.append(functools.reduce(jnp.add, got, kept))
    rows = [jnp.concatenate([part[k] for part in sums]) for k in range(dims["line"])]
    grad = rows[0]
    for k in range(1, dims["line"]):
        grad = grad + shift(rows[k], dims, "line", k)
    new_moment1 = 0.9 * moment1 + 0.1 * grad
    new_moment2 = 0.999 * moment2 + 0.001 * grad * grad
    new_factor = factors[0] - 0.02 * (new_moment1 / (1.0 - 0.9**8)) / (
        jnp.sqrt(new_moment2 / (1.0 - 0.999**8)) + 1e-08
    )
    return (new_factor, new_moment1, new_moment2)


def solution(mesh):
    return jax.shard_map(
        per_device,
        mesh=mesh,
        in_specs=(
            P(AXES, None, None),
            P(None, AXES),
            P(AXES),
            P(),
            P(None, AXES, None),
            P(AXES, None),
            P(AXES, None),
        ),
        out_specs=(P(AXES, None), P(AXES, None), P(AXES, None)),
        check_vma=False,
    )
```

```python
import functools

import jax
import jax.numpy as jnp
from jax import lax
from jax.experimental import pallas as pl
from jax.experimental.pallas import tpu as pltpu
from jax.sharding import PartitionSpec as P

AXES = ("blk", "grp")
CORES = 2
BUFFERS = 5
AHEAD = 3
COPY_PARTS = 4
TILE_J = 16
LAG = 1


def mesh_dims(blk, grp):
    chips = blk // CORES
    inner = 1
    for width in range(1, chips + 1):
        if chips % width == 0 and width * width <= chips:
            inner = width
    return {"outer": chips // inner, "inner": inner, "core": CORES, "line": grp}


def split_index(index, dims):
    line = lax.rem(index, dims["line"])
    rest = lax.div(index, dims["line"])
    core = lax.rem(rest, dims["core"])
    rest = lax.div(rest, dims["core"])
    return {
        "outer": lax.div(rest, dims["inner"]),
        "inner": lax.rem(rest, dims["inner"]),
        "core": core,
        "line": line,
    }


def shift(values, dims, name, step):
    strides = {
        "line": 1,
        "core": dims["line"],
        "inner": dims["line"] * dims["core"],
        "outer": dims["line"] * dims["core"] * dims["inner"],
    }
    total = strides["outer"] * dims["outer"]
    stride, size = strides[name], dims[name]
    perm = []
    for source in range(total):
        at = source // stride % size
        perm.append((source, source + ((at + step) % size - at) * stride))
    return lax.ppermute(values, AXES, perm)


ORDERS = (("outer", "inner"), ("inner", "outer"))


def spread(own, dims, names):
    first, second = names
    own = jnp.concatenate([own] + [shift(own, dims, first, k) for k in range(1, dims[first])])
    return [own] + [shift(own, dims, second, k) for k in range(1, dims[second])]


def gather_rows(shard, dims, extra):
    cut = shard.shape[0] // 2
    parts = (slice(0, cut), slice(cut, None))
    line = [shift(shard, dims, "line", k) for k in range(1, dims["line"])]
    near = [
        jnp.concatenate(spread(shard[part], dims, names)) for part, names in zip(parts, ORDERS)
    ]
    near = [[own, shift(own, dims, "core", 1)] for own in near]
    line, near = lax.optimization_barrier((line, near))
    mids = []
    for part, (first, _) in zip(parts, ORDERS):
        own = jnp.concatenate([piece[part] for piece in line])
        mids.append(
            jnp.concatenate([own] + [shift(own, dims, first, k) for k in range(1, dims[first])])
        )
    mids, extra = lax.optimization_barrier((mids, extra))
    far = []
    for own, (_, second) in zip(mids, ORDERS):
        far.append([own] + [shift(own, dims, second, k) for k in range(1, dims[second])])
    pieces = near[0] + near[1]
    for group in far:
        pieces += group + [shift(piece, dims, "core", 1) for piece in group]
    return pieces, extra


def slots_kernel(dims, local_blocks, piece_count, *refs):
    coords_ref, count_ref, owner_ref, peer_ref, blocks_ref, extra_ref = refs[:6]
    pieces = refs[6 : 6 + piece_count]
    (
        mine_ref,
        other_ref,
        table_ref,
        grad_ref,
        blocks_buf,
        pair_ref,
        model_ref,
        total_ref,
        block_sems,
        piece_sems,
        out_sems,
    ) = refs[6 + piece_count :]
    edge, rank = grad_ref.shape[1], grad_ref.shape[2]
    width = TILE_J * edge
    tiles = edge // TILE_J
    slot_count = blocks_ref.shape[0]
    kept = slot_count - extra_ref.shape[0]
    live = count_ref[0]
    peer_live = peer_ref[3 * slot_count]
    give = jnp.minimum(lax.div(jnp.maximum(live - peer_live, 0), 2), jnp.maximum(live - kept, 0))
    take = jnp.minimum(
        lax.div(jnp.maximum(peer_live - live, 0), 2), jnp.maximum(peer_live - kept, 0)
    )
    mine = live - give
    count = mine + take
    cut = 3 * local_blocks // 2
    here = split_index(lax.axis_index("blk") * dims["line"] + lax.axis_index("grp"), dims)
    columns = dims["core"] * dims["outer"] * dims["inner"] * dims["line"]

    def position(mode, item):
        own = jnp.minimum(item, slot_count - 1)
        other = jnp.clip(item - mine + peer_live - take, 0, slot_count - 1)
        coord = jnp.where(
            item < mine, coords_ref[mode, own], peer_ref[mode * slot_count + other]
        )
        return owner_ref[mode, coord]

    def row_place(mode, item):
        pos = position(mode, item)
        there = split_index(lax.div(pos, local_blocks), dims)
        away = {
            name: lax.rem(here[name] - there[name] + dims[name], dims[name]) for name in dims
        }
        block = mode * local_blocks + lax.rem(pos, local_blocks)
        late = block >= cut
        second = jnp.where(late, away["outer"], away["inner"])
        first = jnp.where(late, away["inner"], away["outer"])
        size_first = jnp.where(late, dims["inner"], dims["outer"])
        size_second = jnp.where(late, dims["outer"], dims["inner"])
        spot = (away["core"] * size_second + second) * size_first + first
        blocks_of = jnp.where(late, 3 * local_blocks - cut, cut)
        inside = jnp.where(late, block - cut, block)
        per_line = columns // dims["line"]
        near = jnp.where(late, per_line * cut, 0) + spot * blocks_of + inside
        others = dims["line"] - 1
        far = jnp.where(late, per_line * others * cut, 0) + per_line * 3 * local_blocks
        far = far + (spot * others + away["line"] - 1) * blocks_of + inside
        return jnp.where(away["line"] == 0, near, far)

    def grad_place(item):
        pos = position(0, item)
        there = split_index(lax.div(pos, local_blocks), dims)
        away = {
            name: lax.rem(there[name] - here[name] + dims[name], dims[name]) for name in dims
        }
        local = lax.rem(pos, local_blocks)
        half_blocks = local_blocks // 2
        late = local >= half_blocks
        second = jnp.where(late, away["outer"], away["inner"])
        first = jnp.where(late, away["inner"], away["outer"])
        size_first = jnp.where(late, dims["inner"], dims["outer"])
        size_second = jnp.where(late, dims["outer"], dims["inner"])
        half = jnp.where(late, 1, 0)
        spot = ((away["core"] * 2 + half) * size_second + second) * size_first + first
        spot = spot * dims["line"] + away["line"]
        return spot * half_blocks + jnp.where(late, local - half_blocks, local)

    def block_copies(source, slot, item):
        at = lax.rem(item, BUFFERS)
        span = edge // COPY_PARTS
        return [
            pltpu.make_async_copy(
                source.at[slot, pl.ds(part * span, span)],
                blocks_buf.at[at, pl.ds(part * span, span)],
                block_sems.at[at, part],
            )
            for part in range(COPY_PARTS)
        ]

    def start(item):
        @pl.when(item < mine)
        def _():
            for copy in block_copies(blocks_ref, item, item):
                copy.start()

        @pl.when((item >= mine) & (item < count))
        def _():
            slot = item - mine + peer_live - take - kept
            for copy in block_copies(extra_ref, slot, item):
                copy.start()

    fills = []
    offset = 0
    for index, piece in enumerate(pieces):
        size = piece.shape[0]
        fills.append(
            pltpu.make_async_copy(
                piece, table_ref.at[pl.ds(offset, size)], piece_sems.at[index]
            )
        )
        offset += size
    for fill in fills:
        fill.start()
    for slot in range(AHEAD):
        start(slot)
    grad_ref[...] = jnp.zeros_like(grad_ref)
    for tile in range(tiles - LAG, tiles):
        pair_ref[tile] = jnp.zeros((width, rank), jnp.bfloat16)
        model_ref[tile] = jnp.zeros((edge, width), jnp.float32)
    total_ref[...] = jnp.zeros_like(total_ref)
    for fill in fills:
        fill.wait()

    def finish(tile, at, total):
        twice = blocks_buf[at, :, tile * width : (tile + 1) * width].astype(jnp.float32) * 2.0
        resid = ((jnp.tanh(model_ref[tile]) + 1.0) - twice).astype(jnp.bfloat16)
        return total + jnp.dot(resid, pair_ref[tile], preferred_element_type=jnp.float32)

    def step(slot, carry):
        start(slot + AHEAD)
        for copy in block_copies(blocks_ref, 0, slot):
            copy.wait()
        at = lax.rem(slot, BUFFERS)
        before = jnp.maximum(slot - 1, 0)
        at_before = lax.rem(before, BUFFERS)
        place_b = row_place(1, slot)
        rows_a = table_ref[row_place(0, slot)] * jnp.asarray(0.5, jnp.bfloat16)
        rows_c = table_ref[row_place(2, slot)]
        total_before = total_ref[...]
        total = jnp.zeros((edge, rank), jnp.float32)
        for tile in range(tiles):
            if tile >= LAG:
                total = finish(tile - LAG, at, total)
            else:
                total_before = finish(tiles - LAG + tile, at_before, total_before)
            pair = jnp.concatenate(
                [
                    table_ref[place_b, pl.ds(tile * TILE_J + j, 1), :] * rows_c
                    for j in range(TILE_J)
                ],
                axis=0,
            )
            pair_ref[tile] = pair
            model_ref[tile] = lax.dot_general(
                rows_a, pair, (((1,), (1,)), ((), ())), preferred_element_type=jnp.float32
            )
        grad_ref[grad_place(before)] += 0.5 * total_before
        total_ref[...] = total
        return carry

    lax.fori_loop(0, count, step, 0)
    last = count - 1
    total = total_ref[...]
    for tile in range(tiles - LAG, tiles):
        total = finish(tile, lax.rem(last, BUFFERS), total)
    grad_ref[grad_place(last)] += 0.5 * total
    half = grad_ref.shape[0] // 2
    for index, out in enumerate((mine_ref, other_ref)):
        pltpu.make_async_copy(
            grad_ref.at[pl.ds(index * half, half)], out, out_sems.at[index]
        ).start()
    for index, out in enumerate((mine_ref, other_ref)):
        pltpu.make_async_copy(
            grad_ref.at[pl.ds(index * half, half)], out, out_sems.at[index]
        ).wait()


def per_device(tensor_blocks, block_coords, block_count, row_owner, factors, moment1, moment2):
    slot_count, edge, width = tensor_blocks.shape
    rank = factors.shape[2]
    local_blocks = moment1.shape[0] // edge
    row_blocks = row_owner.shape[1]
    dims = mesh_dims(lax.axis_size("blk"), lax.axis_size("grp"))
    shard = factors.astype(jnp.bfloat16).reshape(3 * local_blocks, edge, rank)
    sent = slot_count * 7 // 18
    peer = shift(jnp.concatenate([block_coords.reshape(-1), block_count]), dims, "core", 1)
    begin = slot_count - sent + jnp.minimum(peer[3 * slot_count], 0)
    extra = lax.dynamic_slice_in_dim(tensor_blocks, begin, sent, axis=0)
    extra = shift(extra, dims, "core", 1)
    pieces, (extra, peer) = gather_rows(shard, dims, (extra, peer))
    smem = pl.BlockSpec(memory_space=pltpu.SMEM)
    hbm = pl.BlockSpec(memory_space=pl.ANY)
    tiles = edge // TILE_J
    outgoing = jax.ShapeDtypeStruct((row_blocks // 2, edge, rank), jnp.float32)
    mine, other = pl.pallas_call(
        functools.partial(slots_kernel, dims, local_blocks, len(pieces)),
        out_shape=(outgoing, outgoing),
        in_specs=[smem, smem, smem, smem, hbm, hbm] + [hbm] * len(pieces),
        out_specs=(hbm, hbm),
        scratch_shapes=[
            pltpu.VMEM((3 * row_blocks, edge, rank), jnp.bfloat16),
            pltpu.VMEM((row_blocks, edge, rank), jnp.float32),
            pltpu.VMEM((BUFFERS, edge, width), jnp.bfloat16),
            pltpu.VMEM((tiles, TILE_J * edge, rank), jnp.bfloat16),
            pltpu.VMEM((tiles, edge, TILE_J * edge), jnp.float32),
            pltpu.VMEM((edge, rank), jnp.float32),
            pltpu.SemaphoreType.DMA((BUFFERS, COPY_PARTS)),
            pltpu.SemaphoreType.DMA((len(pieces),)),
            pltpu.SemaphoreType.DMA((2,)),
        ],
        compiler_params=pltpu.CompilerParams(vmem_limit_bytes=56 * 1024 * 1024),
        cost_estimate=pl.CostEstimate(
            flops=4 * slot_count * edge * width * rank,
            bytes_accessed=2 * slot_count * edge * width,
            transcendentals=slot_count * edge * width,
        ),
    )(block_coords, block_count, row_owner, peer, tensor_blocks, extra, *pieces)

    def by_half(values):
        values = values.reshape(2, row_blocks // 4, edge, rank)
        out = []
        for half, (first, second) in enumerate(ORDERS):
            out.append(
                values[half].reshape(
                    dims[second], dims[first], dims["line"], local_blocks // 2 * edge, rank
                )
            )
        return out

    arrived = by_half(shift(other, dims, "core", 1))
    kept_halves = by_half(mine)
    sums = []
    for half, (first, second) in enumerate(ORDERS):
        kept, got = kept_halves[half], [arrived[half]]
        for name in (second, first):
            terms = [
                functools.reduce(jnp.add, [g[k] for g in got], kept[k]) for k in range(dims[name])
            ]
            kept = terms[0]
            got = [shift(terms[k], dims, name, k) for k in range(1, dims[name])]
        sums.append(functools.reduce(jnp.add, got, kept))
    rows = [jnp.concatenate([part[k] for part in sums]) for k in range(dims["line"])]
    grad = rows[0]
    for k in range(1, dims["line"]):
        grad = grad + shift(rows[k], dims, "line", k)
    new_moment1 = 0.9 * moment1 + 0.1 * grad
    new_moment2 = 0.999 * moment2 + 0.001 * grad * grad
    new_factor = factors[0] - 0.02 * (new_moment1 / (1.0 - 0.9**8)) / (
        jnp.sqrt(new_moment2 / (1.0 - 0.999**8)) + 1e-08
    )
    return (new_factor, new_moment1, new_moment2)


def solution(mesh):
    return jax.shard_map(
        per_device,
        mesh=mesh,
        in_specs=(
            P(AXES, None, None),
            P(None, AXES),
            P(AXES),
            P(),
            P(None, AXES, None),
            P(AXES, None),
            P(AXES, None),
        ),
        out_specs=(P(AXES, None), P(AXES, None), P(AXES, None)),
        check_vma=False,
    )
```

```python
import functools

import jax
import jax.numpy as jnp
from jax import lax
from jax.experimental import pallas as pl
from jax.experimental.pallas import tpu as pltpu
from jax.sharding import PartitionSpec as P

AXES = ("blk", "grp")
CORES = 2
BUFFERS = 5
AHEAD = 3
COPY_PARTS = 4
TILE_J = 16
LAG = 1


def mesh_dims(blk, grp):
    chips = blk // CORES
    inner = 1
    for width in range(1, chips + 1):
        if chips % width == 0 and width * width <= chips:
            inner = width
    return {"outer": chips // inner, "inner": inner, "core": CORES, "line": grp}


def split_index(index, dims):
    line = lax.rem(index, dims["line"])
    rest = lax.div(index, dims["line"])
    core = lax.rem(rest, dims["core"])
    rest = lax.div(rest, dims["core"])
    return {
        "outer": lax.div(rest, dims["inner"]),
        "inner": lax.rem(rest, dims["inner"]),
        "core": core,
        "line": line,
    }


def shift(values, dims, name, step):
    strides = {
        "line": 1,
        "core": dims["line"],
        "inner": dims["line"] * dims["core"],
        "outer": dims["line"] * dims["core"] * dims["inner"],
    }
    total = strides["outer"] * dims["outer"]
    stride, size = strides[name], dims[name]
    perm = []
    for source in range(total):
        at = source // stride % size
        perm.append((source, source + ((at + step) % size - at) * stride))
    return lax.ppermute(values, AXES, perm)


ORDERS = (("outer", "inner"), ("inner", "outer"))


def gather_rows(shard, dims):
    count = shard.shape[0]
    cut = count // 2
    line = [shard] + [shift(shard, dims, "line", k) for k in range(1, dims["line"])]
    halves = []
    for part, (first, second) in zip((slice(0, cut), slice(cut, count)), ORDERS):
        own = jnp.concatenate([piece[part] for piece in line])
        own = jnp.concatenate([own] + [shift(own, dims, first, k) for k in range(1, dims[first])])
        pieces = [own] + [shift(own, dims, second, k) for k in range(1, dims[second])]
        pieces = pieces + [shift(piece, dims, "core", 1) for piece in pieces]
        halves.append(pieces)
    return halves


def slots_kernel(dims, local_blocks, piece_count, *refs):
    coords_ref, count_ref, owner_ref, peer_ref, blocks_ref, extra_ref = refs[:6]
    pieces = refs[6 : 6 + piece_count]
    (
        mine_ref,
        other_ref,
        table_ref,
        grad_ref,
        blocks_buf,
        pair_ref,
        model_ref,
        total_ref,
        block_sems,
        piece_sems,
        out_sems,
    ) = refs[6 + piece_count :]
    edge, rank = grad_ref.shape[1], grad_ref.shape[2]
    width = TILE_J * edge
    tiles = edge // TILE_J
    slot_count = blocks_ref.shape[0]
    live = count_ref[0]
    peer_live = peer_ref[3 * slot_count]
    give = lax.div(jnp.maximum(live - peer_live, 0), 2)
    take = lax.div(jnp.maximum(peer_live - live, 0), 2)
    mine = live - give
    count = mine + take
    cut = 3 * local_blocks // 2
    here = split_index(lax.axis_index("blk") * dims["line"] + lax.axis_index("grp"), dims)
    columns = dims["core"] * dims["outer"] * dims["inner"] * dims["line"]

    def position(mode, item):
        own = jnp.minimum(item, slot_count - 1)
        other = jnp.clip(item - mine + peer_live - take, 0, slot_count - 1)
        coord = jnp.where(
            item < mine, coords_ref[mode, own], peer_ref[mode * slot_count + other]
        )
        return owner_ref[mode, coord]

    def row_place(mode, item):
        pos = position(mode, item)
        there = split_index(lax.div(pos, local_blocks), dims)
        away = {
            name: lax.rem(here[name] - there[name] + dims[name], dims[name]) for name in dims
        }
        block = mode * local_blocks + lax.rem(pos, local_blocks)
        late = block >= cut
        second = jnp.where(late, away["outer"], away["inner"])
        first = jnp.where(late, away["inner"], away["outer"])
        size_first = jnp.where(late, dims["inner"], dims["outer"])
        size_second = jnp.where(late, dims["outer"], dims["inner"])
        spot = ((away["core"] * size_second + second) * size_first + first) * dims["line"]
        spot = spot + away["line"]
        blocks_of = jnp.where(late, 3 * local_blocks - cut, cut)
        base = jnp.where(late, columns * cut, 0)
        return base + spot * blocks_of + jnp.where(late, block - cut, block)

    def grad_place(item):
        pos = position(0, item)
        there = split_index(lax.div(pos, local_blocks), dims)
        away = {
            name: lax.rem(there[name] - here[name] + dims[name], dims[name]) for name in dims
        }
        local = lax.rem(pos, local_blocks)
        half_blocks = local_blocks // 2
        late = local >= half_blocks
        second = jnp.where(late, away["outer"], away["inner"])
        first = jnp.where(late, away["inner"], away["outer"])
        size_first = jnp.where(late, dims["inner"], dims["outer"])
        size_second = jnp.where(late, dims["outer"], dims["inner"])
        half = jnp.where(late, 1, 0)
        spot = ((away["core"] * 2 + half) * size_second + second) * size_first + first
        spot = spot * dims["line"] + away["line"]
        return spot * half_blocks + jnp.where(late, local - half_blocks, local)

    def block_copies(source, slot, item):
        at = lax.rem(item, BUFFERS)
        span = edge // COPY_PARTS
        return [
            pltpu.make_async_copy(
                source.at[slot, pl.ds(part * span, span)],
                blocks_buf.at[at, pl.ds(part * span, span)],
                block_sems.at[at, part],
            )
            for part in range(COPY_PARTS)
        ]

    def start(item):
        @pl.when(item < mine)
        def _():
            for copy in block_copies(blocks_ref, item, item):
                copy.start()

        @pl.when((item >= mine) & (item < count))
        def _():
            slot = item - mine + peer_live - take
            for copy in block_copies(extra_ref, slot, item):
                copy.start()

    fills = []
    offset = 0
    for index, piece in enumerate(pieces):
        size = piece.shape[0]
        fills.append(
            pltpu.make_async_copy(
                piece, table_ref.at[pl.ds(offset, size)], piece_sems.at[index]
            )
        )
        offset += size
    for fill in fills:
        fill.start()
    for slot in range(AHEAD):
        start(slot)
    grad_ref[...] = jnp.zeros_like(grad_ref)
    for tile in range(tiles - LAG, tiles):
        pair_ref[tile] = jnp.zeros((width, rank), jnp.bfloat16)
        model_ref[tile] = jnp.zeros((edge, width), jnp.float32)
    total_ref[...] = jnp.zeros_like(total_ref)
    for fill in fills:
        fill.wait()

    def finish(tile, at, total):
        twice = blocks_buf[at, :, tile * width : (tile + 1) * width].astype(jnp.float32) * 2.0
        resid = ((jnp.tanh(model_ref[tile]) + 1.0) - twice).astype(jnp.bfloat16)
        return total + jnp.dot(resid, pair_ref[tile], preferred_element_type=jnp.float32)

    def step(slot, carry):
        start(slot + AHEAD)
        for copy in block_copies(blocks_ref, 0, slot):
            copy.wait()
        at = lax.rem(slot, BUFFERS)
        before = jnp.maximum(slot - 1, 0)
        at_before = lax.rem(before, BUFFERS)
        place_b = row_place(1, slot)
        rows_a = table_ref[row_place(0, slot)] * jnp.asarray(0.5, jnp.bfloat16)
        rows_c = table_ref[row_place(2, slot)]
        total_before = total_ref[...]
        total = jnp.zeros((edge, rank), jnp.float32)
        for tile in range(tiles):
            if tile >= LAG:
                total = finish(tile - LAG, at, total)
            else:
                total_before = finish(tiles - LAG + tile, at_before, total_before)
            pair = jnp.concatenate(
                [
                    table_ref[place_b, pl.ds(tile * TILE_J + j, 1), :] * rows_c
                    for j in range(TILE_J)
                ],
                axis=0,
            )
            pair_ref[tile] = pair
            model_ref[tile] = lax.dot_general(
                rows_a, pair, (((1,), (1,)), ((), ())), preferred_element_type=jnp.float32
            )
        grad_ref[grad_place(before)] += 0.5 * total_before
        total_ref[...] = total
        return carry

    lax.fori_loop(0, count, step, 0)
    last = count - 1
    total = total_ref[...]
    for tile in range(tiles - LAG, tiles):
        total = finish(tile, lax.rem(last, BUFFERS), total)
    grad_ref[grad_place(last)] += 0.5 * total
    half = grad_ref.shape[0] // 2
    for index, out in enumerate((mine_ref, other_ref)):
        pltpu.make_async_copy(
            grad_ref.at[pl.ds(index * half, half)], out, out_sems.at[index]
        ).start()
    for index, out in enumerate((mine_ref, other_ref)):
        pltpu.make_async_copy(
            grad_ref.at[pl.ds(index * half, half)], out, out_sems.at[index]
        ).wait()


def per_device(tensor_blocks, block_coords, block_count, row_owner, factors, moment1, moment2):
    slot_count, edge, width = tensor_blocks.shape
    rank = factors.shape[2]
    local_blocks = moment1.shape[0] // edge
    row_blocks = row_owner.shape[1]
    dims = mesh_dims(lax.axis_size("blk"), lax.axis_size("grp"))
    shard = factors.astype(jnp.bfloat16).reshape(3 * local_blocks, edge, rank)
    peer = shift(jnp.concatenate([block_coords.reshape(-1), block_count]), dims, "core", 1)
    extra = shift(tensor_blocks, dims, "core", 1)
    halves = gather_rows(shard, dims)
    pieces = halves[0] + halves[1]
    smem = pl.BlockSpec(memory_space=pltpu.SMEM)
    hbm = pl.BlockSpec(memory_space=pl.ANY)
    tiles = edge // TILE_J
    outgoing = jax.ShapeDtypeStruct((row_blocks // 2, edge, rank), jnp.float32)
    mine, other = pl.pallas_call(
        functools.partial(slots_kernel, dims, local_blocks, len(pieces)),
        out_shape=(outgoing, outgoing),
        in_specs=[smem, smem, smem, smem, hbm, hbm] + [hbm] * len(pieces),
        out_specs=(hbm, hbm),
        scratch_shapes=[
            pltpu.VMEM((3 * row_blocks, edge, rank), jnp.bfloat16),
            pltpu.VMEM((row_blocks, edge, rank), jnp.float32),
            pltpu.VMEM((BUFFERS, edge, width), jnp.bfloat16),
            pltpu.VMEM((tiles, TILE_J * edge, rank), jnp.bfloat16),
            pltpu.VMEM((tiles, edge, TILE_J * edge), jnp.float32),
            pltpu.VMEM((edge, rank), jnp.float32),
            pltpu.SemaphoreType.DMA((BUFFERS, COPY_PARTS)),
            pltpu.SemaphoreType.DMA((len(pieces),)),
            pltpu.SemaphoreType.DMA((2,)),
        ],
        compiler_params=pltpu.CompilerParams(vmem_limit_bytes=56 * 1024 * 1024),
        cost_estimate=pl.CostEstimate(
            flops=4 * slot_count * edge * width * rank,
            bytes_accessed=2 * slot_count * edge * width,
            transcendentals=slot_count * edge * width,
        ),
    )(block_coords, block_count, row_owner, peer, tensor_blocks, extra, *pieces)

    def by_half(values):
        values = values.reshape(2, row_blocks // 4, edge, rank)
        out = []
        for half, (first, second) in enumerate(ORDERS):
            out.append(
                values[half].reshape(
                    dims[second], dims[first], dims["line"], local_blocks // 2 * edge, rank
                )
            )
        return out

    arrived = by_half(shift(other, dims, "core", 1))
    kept_halves = by_half(mine)
    sums = []
    for half, (first, second) in enumerate(ORDERS):
        kept, got = kept_halves[half], [arrived[half]]
        for name in (second, first):
            terms = [
                functools.reduce(jnp.add, [g[k] for g in got], kept[k]) for k in range(dims[name])
            ]
            kept = terms[0]
            got = [shift(terms[k], dims, name, k) for k in range(1, dims[name])]
        sums.append(functools.reduce(jnp.add, got, kept))
    rows = [jnp.concatenate([part[k] for part in sums]) for k in range(dims["line"])]
    grad = rows[0]
    for k in range(1, dims["line"]):
        grad = grad + shift(rows[k], dims, "line", k)
    new_moment1 = 0.9 * moment1 + 0.1 * grad
    new_moment2 = 0.999 * moment2 + 0.001 * grad * grad
    new_factor = factors[0] - 0.02 * (new_moment1 / (1.0 - 0.9**8)) / (
        jnp.sqrt(new_moment2 / (1.0 - 0.999**8)) + 1e-08
    )
    return (new_factor, new_moment1, new_moment2)


def solution(mesh):
    return jax.shard_map(
        per_device,
        mesh=mesh,
        in_specs=(
            P(AXES, None, None),
            P(None, AXES),
            P(AXES),
            P(),
            P(None, AXES, None),
            P(AXES, None),
            P(AXES, None),
        ),
        out_specs=(P(AXES, None), P(AXES, None), P(AXES, None)),
        check_vma=False,
    )
```

```python
import functools

import jax
import jax.numpy as jnp
from jax import lax
from jax.experimental import pallas as pl
from jax.experimental.pallas import tpu as pltpu
from jax.sharding import PartitionSpec as P

AXES = ("blk", "grp")
CORES = 2
BUFFERS = 5
AHEAD = 3
COPY_PARTS = 4
TILE_J = 16
LAG = 1


def mesh_dims(blk, grp):
    chips = blk // CORES
    inner = 1
    for width in range(1, chips + 1):
        if chips % width == 0 and width * width <= chips:
            inner = width
    return {"outer": chips // inner, "inner": inner, "core": CORES, "line": grp}


def split_index(index, dims):
    line = lax.rem(index, dims["line"])
    rest = lax.div(index, dims["line"])
    core = lax.rem(rest, dims["core"])
    rest = lax.div(rest, dims["core"])
    return {
        "outer": lax.div(rest, dims["inner"]),
        "inner": lax.rem(rest, dims["inner"]),
        "core": core,
        "line": line,
    }


def shift(values, dims, name, step):
    strides = {
        "line": 1,
        "core": dims["line"],
        "inner": dims["line"] * dims["core"],
        "outer": dims["line"] * dims["core"] * dims["inner"],
    }
    total = strides["outer"] * dims["outer"]
    stride, size = strides[name], dims[name]
    perm = []
    for source in range(total):
        at = source // stride % size
        perm.append((source, source + ((at + step) % size - at) * stride))
    return lax.ppermute(values, AXES, perm)


ORDERS = (("outer", "inner"), ("inner", "outer"))


def gather_rows(shard, dims):
    cut = shard.shape[0] // 2
    parts = (slice(0, cut), slice(cut, None))
    size = dims["line"]
    early = sorted({1, size - 1} - {0, size})
    line = {k: shift(shard, dims, "line", k) for k in early}
    hops = [
        [shift(shard[part], dims, first, k) for k in range(1, dims[first])]
        for part, (first, _) in zip(parts, ORDERS)
    ]
    shard, line, hops = lax.optimization_barrier((shard, line, hops))
    line.update({k: shift(shard, dims, "line", k) for k in range(1, size) if k not in early})
    near = []
    for part, hop, (_, second) in zip(parts, hops, ORDERS):
        own = jnp.concatenate([shard[part]] + hop)
        near.append([own] + [shift(own, dims, second, k) for k in range(1, dims[second])])
    line, near = lax.optimization_barrier((line, near))
    near = [jnp.concatenate(group) for group in near]
    across = [shift(group, dims, "core", 1) for group in near]
    mids = []
    for part, (first, _) in zip(parts, ORDERS):
        own = jnp.concatenate([line[k][part] for k in range(1, size)])
        mids.append(
            jnp.concatenate([own] + [shift(own, dims, first, k) for k in range(1, dims[first])])
        )
    mids, near, across = lax.optimization_barrier((mids, near, across))
    pieces = [near[0], across[0], near[1], across[1]]
    for own, (_, second) in zip(mids, ORDERS):
        group = [own] + [shift(own, dims, second, k) for k in range(1, dims[second])]
        pieces += group + [shift(piece, dims, "core", 1) for piece in group]
    return pieces


def slots_kernel(dims, local_blocks, piece_count, *refs):
    coords_ref, count_ref, owner_ref, peer_ref, blocks_ref, extra_ref = refs[:6]
    pieces = refs[6 : 6 + piece_count]
    (
        mine_ref,
        other_ref,
        table_ref,
        grad_ref,
        blocks_buf,
        pair_ref,
        model_ref,
        total_ref,
        block_sems,
        piece_sems,
        out_sems,
    ) = refs[6 + piece_count :]
    edge, rank = grad_ref.shape[1], grad_ref.shape[2]
    width = TILE_J * edge
    tiles = edge // TILE_J
    slot_count = blocks_ref.shape[0]
    live = count_ref[0]
    peer_live = peer_ref[3 * slot_count]
    give = lax.div(jnp.maximum(live - peer_live, 0), 2)
    take = lax.div(jnp.maximum(peer_live - live, 0), 2)
    mine = live - give
    count = mine + take
    cut = 3 * local_blocks // 2
    here = split_index(lax.axis_index("blk") * dims["line"] + lax.axis_index("grp"), dims)
    columns = dims["core"] * dims["outer"] * dims["inner"] * dims["line"]

    def position(mode, item):
        own = jnp.minimum(item, slot_count - 1)
        other = jnp.clip(item - mine + peer_live - take, 0, slot_count - 1)
        coord = jnp.where(
            item < mine, coords_ref[mode, own], peer_ref[mode * slot_count + other]
        )
        return owner_ref[mode, coord]

    def row_place(mode, item):
        pos = position(mode, item)
        there = split_index(lax.div(pos, local_blocks), dims)
        away = {
            name: lax.rem(here[name] - there[name] + dims[name], dims[name]) for name in dims
        }
        block = mode * local_blocks + lax.rem(pos, local_blocks)
        late = block >= cut
        second = jnp.where(late, away["outer"], away["inner"])
        first = jnp.where(late, away["inner"], away["outer"])
        size_first = jnp.where(late, dims["inner"], dims["outer"])
        size_second = jnp.where(late, dims["outer"], dims["inner"])
        spot = (away["core"] * size_second + second) * size_first + first
        blocks_of = jnp.where(late, 3 * local_blocks - cut, cut)
        inside = jnp.where(late, block - cut, block)
        per_line = columns // dims["line"]
        near = jnp.where(late, per_line * cut, 0) + spot * blocks_of + inside
        others = dims["line"] - 1
        far = jnp.where(late, per_line * others * cut, 0) + per_line * 3 * local_blocks
        far = far + (spot * others + away["line"] - 1) * blocks_of + inside
        return jnp.where(away["line"] == 0, near, far)

    def grad_place(item):
        pos = position(0, item)
        there = split_index(lax.div(pos, local_blocks), dims)
        away = {
            name: lax.rem(there[name] - here[name] + dims[name], dims[name]) for name in dims
        }
        local = lax.rem(pos, local_blocks)
        half_blocks = local_blocks // 2
        late = local >= half_blocks
        second = jnp.where(late, away["outer"], away["inner"])
        first = jnp.where(late, away["inner"], away["outer"])
        size_first = jnp.where(late, dims["inner"], dims["outer"])
        size_second = jnp.where(late, dims["outer"], dims["inner"])
        half = jnp.where(late, 1, 0)
        spot = ((away["core"] * 2 + half) * size_second + second) * size_first + first
        spot = spot * dims["line"] + away["line"]
        return spot * half_blocks + jnp.where(late, local - half_blocks, local)

    def block_copies(source, slot, item):
        at = lax.rem(item, BUFFERS)
        span = edge // COPY_PARTS
        return [
            pltpu.make_async_copy(
                source.at[slot, pl.ds(part * span, span)],
                blocks_buf.at[at, pl.ds(part * span, span)],
                block_sems.at[at, part],
            )
            for part in range(COPY_PARTS)
        ]

    def start(item):
        @pl.when(item < mine)
        def _():
            for copy in block_copies(blocks_ref, item, item):
                copy.start()

        @pl.when((item >= mine) & (item < count))
        def _():
            slot = item - mine + peer_live - take
            for copy in block_copies(extra_ref, slot, item):
                copy.start()

    fills = []
    offset = 0
    for index, piece in enumerate(pieces):
        size = piece.shape[0]
        fills.append(
            pltpu.make_async_copy(
                piece, table_ref.at[pl.ds(offset, size)], piece_sems.at[index]
            )
        )
        offset += size
    for fill in fills:
        fill.start()
    for slot in range(AHEAD):
        start(slot)
    grad_ref[...] = jnp.zeros_like(grad_ref)
    for tile in range(tiles - LAG, tiles):
        pair_ref[tile] = jnp.zeros((width, rank), jnp.bfloat16)
        model_ref[tile] = jnp.zeros((edge, width), jnp.float32)
    total_ref[...] = jnp.zeros_like(total_ref)
    for fill in fills:
        fill.wait()

    def finish(tile, at, total):
        twice = blocks_buf[at, :, tile * width : (tile + 1) * width].astype(jnp.float32) * 2.0
        resid = ((jnp.tanh(model_ref[tile]) + 1.0) - twice).astype(jnp.bfloat16)
        return total + jnp.dot(resid, pair_ref[tile], preferred_element_type=jnp.float32)

    def step(slot, carry):
        start(slot + AHEAD)
        for copy in block_copies(blocks_ref, 0, slot):
            copy.wait()
        at = lax.rem(slot, BUFFERS)
        before = jnp.maximum(slot - 1, 0)
        at_before = lax.rem(before, BUFFERS)
        place_b = row_place(1, slot)
        rows_a = table_ref[row_place(0, slot)] * jnp.asarray(0.5, jnp.bfloat16)
        rows_c = table_ref[row_place(2, slot)]
        total_before = total_ref[...]
        total = jnp.zeros((edge, rank), jnp.float32)
        for tile in range(tiles):
            if tile >= LAG:
                total = finish(tile - LAG, at, total)
            else:
                total_before = finish(tiles - LAG + tile, at_before, total_before)
            pair = jnp.concatenate(
                [
                    table_ref[place_b, pl.ds(tile * TILE_J + j, 1), :] * rows_c
                    for j in range(TILE_J)
                ],
                axis=0,
            )
            pair_ref[tile] = pair
            model_ref[tile] = lax.dot_general(
                rows_a, pair, (((1,), (1,)), ((), ())), preferred_element_type=jnp.float32
            )
        grad_ref[grad_place(before)] += 0.5 * total_before
        total_ref[...] = total
        return carry

    lax.fori_loop(0, count, step, 0)
    last = count - 1
    total = total_ref[...]
    for tile in range(tiles - LAG, tiles):
        total = finish(tile, lax.rem(last, BUFFERS), total)
    grad_ref[grad_place(last)] += 0.5 * total
    half = grad_ref.shape[0] // 2
    for index, out in enumerate((mine_ref, other_ref)):
        pltpu.make_async_copy(
            grad_ref.at[pl.ds(index * half, half)], out, out_sems.at[index]
        ).start()
    for index, out in enumerate((mine_ref, other_ref)):
        pltpu.make_async_copy(
            grad_ref.at[pl.ds(index * half, half)], out, out_sems.at[index]
        ).wait()


def per_device(tensor_blocks, block_coords, block_count, row_owner, factors, moment1, moment2):
    slot_count, edge, width = tensor_blocks.shape
    rank = factors.shape[2]
    local_blocks = moment1.shape[0] // edge
    row_blocks = row_owner.shape[1]
    dims = mesh_dims(lax.axis_size("blk"), lax.axis_size("grp"))
    shard = factors.astype(jnp.bfloat16).reshape(3 * local_blocks, edge, rank)
    peer = shift(jnp.concatenate([block_coords.reshape(-1), block_count]), dims, "core", 1)
    extra = shift(tensor_blocks, dims, "core", 1)
    pieces = gather_rows(shard, dims)
    smem = pl.BlockSpec(memory_space=pltpu.SMEM)
    hbm = pl.BlockSpec(memory_space=pl.ANY)
    tiles = edge // TILE_J
    outgoing = jax.ShapeDtypeStruct((row_blocks // 2, edge, rank), jnp.float32)
    mine, other = pl.pallas_call(
        functools.partial(slots_kernel, dims, local_blocks, len(pieces)),
        out_shape=(outgoing, outgoing),
        in_specs=[smem, smem, smem, smem, hbm, hbm] + [hbm] * len(pieces),
        out_specs=(hbm, hbm),
        scratch_shapes=[
            pltpu.VMEM((3 * row_blocks, edge, rank), jnp.bfloat16),
            pltpu.VMEM((row_blocks, edge, rank), jnp.float32),
            pltpu.VMEM((BUFFERS, edge, width), jnp.bfloat16),
            pltpu.VMEM((tiles, TILE_J * edge, rank), jnp.bfloat16),
            pltpu.VMEM((tiles, edge, TILE_J * edge), jnp.float32),
            pltpu.VMEM((edge, rank), jnp.float32),
            pltpu.SemaphoreType.DMA((BUFFERS, COPY_PARTS)),
            pltpu.SemaphoreType.DMA((len(pieces),)),
            pltpu.SemaphoreType.DMA((2,)),
        ],
        compiler_params=pltpu.CompilerParams(vmem_limit_bytes=56 * 1024 * 1024),
        cost_estimate=pl.CostEstimate(
            flops=4 * slot_count * edge * width * rank,
            bytes_accessed=2 * slot_count * edge * width,
            transcendentals=slot_count * edge * width,
        ),
    )(block_coords, block_count, row_owner, peer, tensor_blocks, extra, *pieces)

    def by_half(values):
        values = values.reshape(2, row_blocks // 4, edge, rank)
        out = []
        for half, (first, second) in enumerate(ORDERS):
            out.append(
                values[half].reshape(
                    dims[second], dims[first], dims["line"], local_blocks // 2 * edge, rank
                )
            )
        return out

    arrived = by_half(shift(other, dims, "core", 1))
    kept_halves = by_half(mine)
    sums = []
    for half, (first, second) in enumerate(ORDERS):
        kept, got = kept_halves[half], [arrived[half]]
        for name in (second, first):
            terms = [
                functools.reduce(jnp.add, [g[k] for g in got], kept[k]) for k in range(dims[name])
            ]
            kept = terms[0]
            got = [shift(terms[k], dims, name, k) for k in range(1, dims[name])]
        sums.append(functools.reduce(jnp.add, got, kept))
    rows = [jnp.concatenate([part[k] for part in sums]) for k in range(dims["line"])]
    grad = rows[0]
    for k in range(1, dims["line"]):
        grad = grad + shift(rows[k], dims, "line", k)
    new_moment1 = 0.9 * moment1 + 0.1 * grad
    new_moment2 = 0.999 * moment2 + 0.001 * grad * grad
    new_factor = factors[0] - 0.02 * (new_moment1 / (1.0 - 0.9**8)) / (
        jnp.sqrt(new_moment2 / (1.0 - 0.999**8)) + 1e-08
    )
    return (new_factor, new_moment1, new_moment2)


def solution(mesh):
    return jax.shard_map(
        per_device,
        mesh=mesh,
        in_specs=(
            P(AXES, None, None),
            P(None, AXES),
            P(AXES),
            P(),
            P(None, AXES, None),
            P(AXES, None),
            P(AXES, None),
        ),
        out_specs=(P(AXES, None), P(AXES, None), P(AXES, None)),
        check_vma=False,
    )
```

```python
import functools

import jax
import jax.numpy as jnp
from jax import lax
from jax.experimental import pallas as pl
from jax.experimental.pallas import tpu as pltpu
from jax.sharding import PartitionSpec as P

AXES = ("blk", "grp")
CORES = 2
BUFFERS = 5
AHEAD = 3
COPY_PARTS = 4
TILE_J = 16
LAG = 1


def mesh_dims(blk, grp):
    chips = blk // CORES
    inner = 1
    for width in range(1, chips + 1):
        if chips % width == 0 and width * width <= chips:
            inner = width
    return {"outer": chips // inner, "inner": inner, "core": CORES, "line": grp}


def split_index(index, dims):
    line = lax.rem(index, dims["line"])
    rest = lax.div(index, dims["line"])
    core = lax.rem(rest, dims["core"])
    rest = lax.div(rest, dims["core"])
    return {
        "outer": lax.div(rest, dims["inner"]),
        "inner": lax.rem(rest, dims["inner"]),
        "core": core,
        "line": line,
    }


def shift(values, dims, name, step):
    strides = {
        "line": 1,
        "core": dims["line"],
        "inner": dims["line"] * dims["core"],
        "outer": dims["line"] * dims["core"] * dims["inner"],
    }
    total = strides["outer"] * dims["outer"]
    stride, size = strides[name], dims[name]
    perm = []
    for source in range(total):
        at = source // stride % size
        perm.append((source, source + ((at + step) % size - at) * stride))
    return lax.ppermute(values, AXES, perm)


ORDERS = (("outer", "inner"), ("inner", "outer"))


def gather_rows(shard, dims):
    cut = shard.shape[0] // 2
    parts = (slice(0, cut), slice(cut, None))
    size = dims["line"]
    line = [shift(shard, dims, "line", k) for k in range(1, size)]
    hops = [
        [shift(shard[part], dims, first, k) for k in range(1, dims[first])]
        for part, (first, _) in zip(parts, ORDERS)
    ]
    line, hops = lax.optimization_barrier((line, hops))
    near = []
    for part, hop, (_, second) in zip(parts, hops, ORDERS):
        own = jnp.concatenate([shard[part]] + hop)
        near.append([own] + [shift(own, dims, second, k) for k in range(1, dims[second])])
    mids = []
    for part, (first, _) in zip(parts, ORDERS):
        own = jnp.concatenate([piece[part] for piece in line])
        mids.append(
            jnp.concatenate([own] + [shift(own, dims, first, k) for k in range(1, dims[first])])
        )
    mids, near = lax.optimization_barrier((mids, near))
    near = [jnp.concatenate(group) for group in near]
    across = [shift(group, dims, "core", 1) for group in near]
    pieces = [near[0], across[0], near[1], across[1]]
    for own, (_, second) in zip(mids, ORDERS):
        group = [own] + [shift(own, dims, second, k) for k in range(1, dims[second])]
        pieces += group + [shift(piece, dims, "core", 1) for piece in group]
    return pieces


def slots_kernel(dims, local_blocks, piece_count, *refs):
    coords_ref, count_ref, owner_ref, peer_ref, blocks_ref, extra_ref = refs[:6]
    pieces = refs[6 : 6 + piece_count]
    (
        mine_ref,
        other_ref,
        table_ref,
        grad_ref,
        blocks_buf,
        pair_ref,
        model_ref,
        total_ref,
        block_sems,
        piece_sems,
        out_sems,
    ) = refs[6 + piece_count :]
    edge, rank = grad_ref.shape[1], grad_ref.shape[2]
    width = TILE_J * edge
    tiles = edge // TILE_J
    slot_count = blocks_ref.shape[0]
    live = count_ref[0]
    peer_live = peer_ref[3 * slot_count]
    give = lax.div(jnp.maximum(live - peer_live, 0), 2)
    take = lax.div(jnp.maximum(peer_live - live, 0), 2)
    mine = live - give
    count = mine + take
    cut = 3 * local_blocks // 2
    here = split_index(lax.axis_index("blk") * dims["line"] + lax.axis_index("grp"), dims)
    columns = dims["core"] * dims["outer"] * dims["inner"] * dims["line"]

    def position(mode, item):
        own = jnp.minimum(item, slot_count - 1)
        other = jnp.clip(item - mine + peer_live - take, 0, slot_count - 1)
        coord = jnp.where(
            item < mine, coords_ref[mode, own], peer_ref[mode * slot_count + other]
        )
        return owner_ref[mode, coord]

    def row_place(mode, item):
        pos = position(mode, item)
        there = split_index(lax.div(pos, local_blocks), dims)
        away = {
            name: lax.rem(here[name] - there[name] + dims[name], dims[name]) for name in dims
        }
        block = mode * local_blocks + lax.rem(pos, local_blocks)
        late = block >= cut
        second = jnp.where(late, away["outer"], away["inner"])
        first = jnp.where(late, away["inner"], away["outer"])
        size_first = jnp.where(late, dims["inner"], dims["outer"])
        size_second = jnp.where(late, dims["outer"], dims["inner"])
        spot = (away["core"] * size_second + second) * size_first + first
        blocks_of = jnp.where(late, 3 * local_blocks - cut, cut)
        inside = jnp.where(late, block - cut, block)
        per_line = columns // dims["line"]
        near = jnp.where(late, per_line * cut, 0) + spot * blocks_of + inside
        others = dims["line"] - 1
        far = jnp.where(late, per_line * others * cut, 0) + per_line * 3 * local_blocks
        far = far + (spot * others + away["line"] - 1) * blocks_of + inside
        return jnp.where(away["line"] == 0, near, far)

    def grad_place(item):
        pos = position(0, item)
        there = split_index(lax.div(pos, local_blocks), dims)
        away = {
            name: lax.rem(there[name] - here[name] + dims[name], dims[name]) for name in dims
        }
        local = lax.rem(pos, local_blocks)
        half_blocks = local_blocks // 2
        late = local >= half_blocks
        second = jnp.where(late, away["outer"], away["inner"])
        first = jnp.where(late, away["inner"], away["outer"])
        size_first = jnp.where(late, dims["inner"], dims["outer"])
        size_second = jnp.where(late, dims["outer"], dims["inner"])
        half = jnp.where(late, 1, 0)
        spot = ((away["core"] * 2 + half) * size_second + second) * size_first + first
        spot = spot * dims["line"] + away["line"]
        return spot * half_blocks + jnp.where(late, local - half_blocks, local)

    def block_copies(source, slot, item):
        at = lax.rem(item, BUFFERS)
        span = edge // COPY_PARTS
        return [
            pltpu.make_async_copy(
                source.at[slot, pl.ds(part * span, span)],
                blocks_buf.at[at, pl.ds(part * span, span)],
                block_sems.at[at, part],
            )
            for part in range(COPY_PARTS)
        ]

    def start(item):
        @pl.when(item < mine)
        def _():
            for copy in block_copies(blocks_ref, item, item):
                copy.start()

        @pl.when((item >= mine) & (item < count))
        def _():
            slot = item - mine + peer_live - take
            for copy in block_copies(extra_ref, slot, item):
                copy.start()

    fills = []
    offset = 0
    for index, piece in enumerate(pieces):
        size = piece.shape[0]
        fills.append(
            pltpu.make_async_copy(
                piece, table_ref.at[pl.ds(offset, size)], piece_sems.at[index]
            )
        )
        offset += size
    for slot in range(AHEAD):
        start(slot)
    for fill in fills:
        fill.start()
    grad_ref[...] = jnp.zeros_like(grad_ref)
    for tile in range(tiles - LAG, tiles):
        pair_ref[tile] = jnp.zeros((width, rank), jnp.bfloat16)
        model_ref[tile] = jnp.zeros((edge, width), jnp.float32)
    total_ref[...] = jnp.zeros_like(total_ref)
    for fill in fills:
        fill.wait()

    def finish(tile, at, total):
        twice = blocks_buf[at, :, tile * width : (tile + 1) * width].astype(jnp.float32) * 2.0
        resid = ((jnp.tanh(model_ref[tile]) + 1.0) - twice).astype(jnp.bfloat16)
        return total + jnp.dot(resid, pair_ref[tile], preferred_element_type=jnp.float32)

    def step(slot, carry):
        start(slot + AHEAD)
        for copy in block_copies(blocks_ref, 0, slot):
            copy.wait()
        at = lax.rem(slot, BUFFERS)
        before = jnp.maximum(slot - 1, 0)
        at_before = lax.rem(before, BUFFERS)
        place_b = row_place(1, slot)
        rows_a = table_ref[row_place(0, slot)] * jnp.asarray(0.5, jnp.bfloat16)
        rows_c = table_ref[row_place(2, slot)]
        total_before = total_ref[...]
        total = jnp.zeros((edge, rank), jnp.float32)
        for tile in range(tiles):
            if tile >= LAG:
                total = finish(tile - LAG, at, total)
            else:
                total_before = finish(tiles - LAG + tile, at_before, total_before)
            pair = jnp.concatenate(
                [
                    table_ref[place_b, pl.ds(tile * TILE_J + j, 1), :] * rows_c
                    for j in range(TILE_J)
                ],
                axis=0,
            )
            pair_ref[tile] = pair
            model_ref[tile] = lax.dot_general(
                rows_a, pair, (((1,), (1,)), ((), ())), preferred_element_type=jnp.float32
            )
        grad_ref[grad_place(before)] += 0.5 * total_before
        total_ref[...] = total
        return carry

    lax.fori_loop(0, count, step, 0)
    last = count - 1
    total = total_ref[...]
    for tile in range(tiles - LAG, tiles):
        total = finish(tile, lax.rem(last, BUFFERS), total)
    grad_ref[grad_place(last)] += 0.5 * total
    half = grad_ref.shape[0] // 2
    for index, out in enumerate((mine_ref, other_ref)):
        pltpu.make_async_copy(
            grad_ref.at[pl.ds(index * half, half)], out, out_sems.at[index]
        ).start()
    for index, out in enumerate((mine_ref, other_ref)):
        pltpu.make_async_copy(
            grad_ref.at[pl.ds(index * half, half)], out, out_sems.at[index]
        ).wait()


def per_device(tensor_blocks, block_coords, block_count, row_owner, factors, moment1, moment2):
    slot_count, edge, width = tensor_blocks.shape
    rank = factors.shape[2]
    local_blocks = moment1.shape[0] // edge
    row_blocks = row_owner.shape[1]
    dims = mesh_dims(lax.axis_size("blk"), lax.axis_size("grp"))
    shard = factors.astype(jnp.bfloat16).reshape(3 * local_blocks, edge, rank)
    peer = shift(jnp.concatenate([block_coords.reshape(-1), block_count]), dims, "core", 1)
    extra = shift(tensor_blocks, dims, "core", 1)
    pieces = gather_rows(shard, dims)
    smem = pl.BlockSpec(memory_space=pltpu.SMEM)
    hbm = pl.BlockSpec(memory_space=pl.ANY)
    tiles = edge // TILE_J
    outgoing = jax.ShapeDtypeStruct((row_blocks // 2, edge, rank), jnp.float32)
    mine, other = pl.pallas_call(
        functools.partial(slots_kernel, dims, local_blocks, len(pieces)),
        out_shape=(outgoing, outgoing),
        in_specs=[smem, smem, smem, smem, hbm, hbm] + [hbm] * len(pieces),
        out_specs=(hbm, hbm),
        scratch_shapes=[
            pltpu.VMEM((3 * row_blocks, edge, rank), jnp.bfloat16),
            pltpu.VMEM((row_blocks, edge, rank), jnp.float32),
            pltpu.VMEM((BUFFERS, edge, width), jnp.bfloat16),
            pltpu.VMEM((tiles, TILE_J * edge, rank), jnp.bfloat16),
            pltpu.VMEM((tiles, edge, TILE_J * edge), jnp.float32),
            pltpu.VMEM((edge, rank), jnp.float32),
            pltpu.SemaphoreType.DMA((BUFFERS, COPY_PARTS)),
            pltpu.SemaphoreType.DMA((len(pieces),)),
            pltpu.SemaphoreType.DMA((2,)),
        ],
        compiler_params=pltpu.CompilerParams(vmem_limit_bytes=56 * 1024 * 1024),
        cost_estimate=pl.CostEstimate(
            flops=4 * slot_count * edge * width * rank,
            bytes_accessed=2 * slot_count * edge * width,
            transcendentals=slot_count * edge * width,
        ),
    )(block_coords, block_count, row_owner, peer, tensor_blocks, extra, *pieces)

    def by_half(values):
        values = values.reshape(2, row_blocks // 4, edge, rank)
        out = []
        for half, (first, second) in enumerate(ORDERS):
            out.append(
                values[half].reshape(
                    dims[second], dims[first], dims["line"], local_blocks // 2 * edge, rank
                )
            )
        return out

    arrived = by_half(shift(other, dims, "core", 1))
    kept_halves = by_half(mine)
    sums = []
    for half, (first, second) in enumerate(ORDERS):
        kept, got = kept_halves[half], [arrived[half]]
        for name in (second, first):
            terms = [
                functools.reduce(jnp.add, [g[k] for g in got], kept[k]) for k in range(dims[name])
            ]
            kept = terms[0]
            got = [shift(terms[k], dims, name, k) for k in range(1, dims[name])]
        sums.append(functools.reduce(jnp.add, got, kept))
    rows = [jnp.concatenate([part[k] for part in sums]) for k in range(dims["line"])]
    grad = rows[0]
    for k in range(1, dims["line"]):
        grad = grad + shift(rows[k], dims, "line", k)
    new_moment1 = 0.9 * moment1 + 0.1 * grad
    new_moment2 = 0.999 * moment2 + 0.001 * grad * grad
    new_factor = factors[0] - 0.02 * (new_moment1 / (1.0 - 0.9**8)) / (
        jnp.sqrt(new_moment2 / (1.0 - 0.999**8)) + 1e-08
    )
    return (new_factor, new_moment1, new_moment2)


def solution(mesh):
    return jax.shard_map(
        per_device,
        mesh=mesh,
        in_specs=(
            P(AXES, None, None),
            P(None, AXES),
            P(AXES),
            P(),
            P(None, AXES, None),
            P(AXES, None),
            P(AXES, None),
        ),
        out_specs=(P(AXES, None), P(AXES, None), P(AXES, None)),
        check_vma=False,
    )
```

```python
import functools

import jax
import jax.numpy as jnp
from jax import lax
from jax.experimental import pallas as pl
from jax.experimental.pallas import tpu as pltpu
from jax.sharding import PartitionSpec as P

AXES = ("blk", "grp")
CORES = 2
BUFFERS = 5
AHEAD = 3
COPY_PARTS = 4
TILE_J = 16
LAG = 1


def mesh_dims(blk, grp):
    chips = blk // CORES
    inner = 1
    for width in range(1, chips + 1):
        if chips % width == 0 and width * width <= chips:
            inner = width
    return {"outer": chips // inner, "inner": inner, "core": CORES, "line": grp}


def split_index(index, dims):
    line = lax.rem(index, dims["line"])
    rest = lax.div(index, dims["line"])
    core = lax.rem(rest, dims["core"])
    rest = lax.div(rest, dims["core"])
    return {
        "outer": lax.div(rest, dims["inner"]),
        "inner": lax.rem(rest, dims["inner"]),
        "core": core,
        "line": line,
    }


def shift(values, dims, name, step):
    strides = {
        "line": 1,
        "core": dims["line"],
        "inner": dims["line"] * dims["core"],
        "outer": dims["line"] * dims["core"] * dims["inner"],
    }
    total = strides["outer"] * dims["outer"]
    stride, size = strides[name], dims[name]
    perm = []
    for source in range(total):
        at = source // stride % size
        perm.append((source, source + ((at + step) % size - at) * stride))
    return lax.ppermute(values, AXES, perm)


ORDERS = (("outer", "inner"), ("inner", "outer"))


def gather_rows(shard, dims):
    cut = shard.shape[0] // 2
    parts = (slice(0, cut), slice(cut, None))
    size = dims["line"]
    early = sorted({1, size - 1} - {0, size})
    line = {k: shift(shard, dims, "line", k) for k in early}
    hops = [
        [shift(shard[part], dims, first, k) for k in range(1, dims[first])]
        for part, (first, _) in zip(parts, ORDERS)
    ]
    late = {k: shift(shard, dims, "line", k) for k in range(1, size) if k not in early}
    shard, line, hops = lax.optimization_barrier((shard, line, hops))
    line.update(late)
    near = []
    for part, hop, (_, second) in zip(parts, hops, ORDERS):
        own = jnp.concatenate([shard[part]] + hop)
        near.append([own] + [shift(own, dims, second, k) for k in range(1, dims[second])])
    line, near = lax.optimization_barrier((line, near))
    near = [jnp.concatenate(group) for group in near]
    across = [shift(group, dims, "core", 1) for group in near]
    mids = []
    for part, (first, _) in zip(parts, ORDERS):
        own = jnp.concatenate([line[k][part] for k in range(1, size)])
        mids.append(
            jnp.concatenate([own] + [shift(own, dims, first, k) for k in range(1, dims[first])])
        )
    mids, near, across = lax.optimization_barrier((mids, near, across))
    pieces = [near[0], across[0], near[1], across[1]]
    for own, (_, second) in zip(mids, ORDERS):
        group = [own] + [shift(own, dims, second, k) for k in range(1, dims[second])]
        pieces += group + [shift(piece, dims, "core", 1) for piece in group]
    return pieces


def slots_kernel(dims, local_blocks, piece_count, *refs):
    coords_ref, count_ref, owner_ref, peer_ref, blocks_ref, extra_ref = refs[:6]
    pieces = refs[6 : 6 + piece_count]
    (
        mine_ref,
        other_ref,
        table_ref,
        grad_ref,
        blocks_buf,
        pair_ref,
        model_ref,
        total_ref,
        block_sems,
        piece_sems,
        out_sems,
    ) = refs[6 + piece_count :]
    edge, rank = grad_ref.shape[1], grad_ref.shape[2]
    width = TILE_J * edge
    tiles = edge // TILE_J
    slot_count = blocks_ref.shape[0]
    live = count_ref[0]
    peer_live = peer_ref[3 * slot_count]
    give = lax.div(jnp.maximum(live - peer_live, 0), 2)
    take = lax.div(jnp.maximum(peer_live - live, 0), 2)
    mine = live - give
    count = mine + take
    cut = 3 * local_blocks // 2
    here = split_index(lax.axis_index("blk") * dims["line"] + lax.axis_index("grp"), dims)
    columns = dims["core"] * dims["outer"] * dims["inner"] * dims["line"]

    def position(mode, item):
        own = jnp.minimum(item, slot_count - 1)
        other = jnp.clip(item - mine + peer_live - take, 0, slot_count - 1)
        coord = jnp.where(
            item < mine, coords_ref[mode, own], peer_ref[mode * slot_count + other]
        )
        return owner_ref[mode, coord]

    def row_place(mode, item):
        pos = position(mode, item)
        there = split_index(lax.div(pos, local_blocks), dims)
        away = {
            name: lax.rem(here[name] - there[name] + dims[name], dims[name]) for name in dims
        }
        block = mode * local_blocks + lax.rem(pos, local_blocks)
        late = block >= cut
        second = jnp.where(late, away["outer"], away["inner"])
        first = jnp.where(late, away["inner"], away["outer"])
        size_first = jnp.where(late, dims["inner"], dims["outer"])
        size_second = jnp.where(late, dims["outer"], dims["inner"])
        spot = (away["core"] * size_second + second) * size_first + first
        blocks_of = jnp.where(late, 3 * local_blocks - cut, cut)
        inside = jnp.where(late, block - cut, block)
        per_line = columns // dims["line"]
        near = jnp.where(late, per_line * cut, 0) + spot * blocks_of + inside
        others = dims["line"] - 1
        far = jnp.where(late, per_line * others * cut, 0) + per_line * 3 * local_blocks
        far = far + (spot * others + away["line"] - 1) * blocks_of + inside
        return jnp.where(away["line"] == 0, near, far)

    def grad_place(item):
        pos = position(0, item)
        there = split_index(lax.div(pos, local_blocks), dims)
        away = {
            name: lax.rem(there[name] - here[name] + dims[name], dims[name]) for name in dims
        }
        local = lax.rem(pos, local_blocks)
        half_blocks = local_blocks // 2
        late = local >= half_blocks
        second = jnp.where(late, away["outer"], away["inner"])
        first = jnp.where(late, away["inner"], away["outer"])
        size_first = jnp.where(late, dims["inner"], dims["outer"])
        size_second = jnp.where(late, dims["outer"], dims["inner"])
        half = jnp.where(late, 1, 0)
        spot = ((away["core"] * 2 + half) * size_second + second) * size_first + first
        spot = spot * dims["line"] + away["line"]
        return spot * half_blocks + jnp.where(late, local - half_blocks, local)

    def block_copies(source, slot, item):
        at = lax.rem(item, BUFFERS)
        span = edge // COPY_PARTS
        return [
            pltpu.make_async_copy(
                source.at[slot, pl.ds(part * span, span)],
                blocks_buf.at[at, pl.ds(part * span, span)],
                block_sems.at[at, part],
            )
            for part in range(COPY_PARTS)
        ]

    def start(item):
        @pl.when(item < mine)
        def _():
            for copy in block_copies(blocks_ref, item, item):
                copy.start()

        @pl.when((item >= mine) & (item < count))
        def _():
            slot = item - mine + peer_live - take
            for copy in block_copies(extra_ref, slot, item):
                copy.start()

    fills = []
    offset = 0
    for index, piece in enumerate(pieces):
        size = piece.shape[0]
        fills.append(
            pltpu.make_async_copy(
                piece, table_ref.at[pl.ds(offset, size)], piece_sems.at[index]
            )
        )
        offset += size
    for slot in range(AHEAD):
        start(slot)
    for fill in fills:
        fill.start()
    grad_ref[...] = jnp.zeros_like(grad_ref)
    for tile in range(tiles - LAG, tiles):
        pair_ref[tile] = jnp.zeros((width, rank), jnp.bfloat16)
        model_ref[tile] = jnp.zeros((edge, width), jnp.float32)
    total_ref[...] = jnp.zeros_like(total_ref)
    for fill in fills:
        fill.wait()

    def finish(tile, at, total):
        twice = blocks_buf[at, :, tile * width : (tile + 1) * width].astype(jnp.float32) * 2.0
        resid = ((jnp.tanh(model_ref[tile]) + 1.0) - twice).astype(jnp.bfloat16)
        return total + jnp.dot(resid, pair_ref[tile], preferred_element_type=jnp.float32)

    def step(slot, carry):
        start(slot + AHEAD)
        for copy in block_copies(blocks_ref, 0, slot):
            copy.wait()
        at = lax.rem(slot, BUFFERS)
        before = jnp.maximum(slot - 1, 0)
        at_before = lax.rem(before, BUFFERS)
        place_b = row_place(1, slot)
        rows_a = table_ref[row_place(0, slot)] * jnp.asarray(0.5, jnp.bfloat16)
        rows_c = table_ref[row_place(2, slot)]
        total_before = total_ref[...]
        total = jnp.zeros((edge, rank), jnp.float32)
        for tile in range(tiles):
            if tile >= LAG:
                total = finish(tile - LAG, at, total)
            else:
                total_before = finish(tiles - LAG + tile, at_before, total_before)
            pair = jnp.concatenate(
                [
                    table_ref[place_b, pl.ds(tile * TILE_J + j, 1), :] * rows_c
                    for j in range(TILE_J)
                ],
                axis=0,
            )
            pair_ref[tile] = pair
            model_ref[tile] = lax.dot_general(
                rows_a, pair, (((1,), (1,)), ((), ())), preferred_element_type=jnp.float32
            )
        grad_ref[grad_place(before)] += 0.5 * total_before
        total_ref[...] = total
        return carry

    lax.fori_loop(0, count, step, 0)
    last = count - 1
    total = total_ref[...]
    for tile in range(tiles - LAG, tiles):
        total = finish(tile, lax.rem(last, BUFFERS), total)
    grad_ref[grad_place(last)] += 0.5 * total
    half = grad_ref.shape[0] // 2
    for index, out in enumerate((mine_ref, other_ref)):
        pltpu.make_async_copy(
            grad_ref.at[pl.ds(index * half, half)], out, out_sems.at[index]
        ).start()
    for index, out in enumerate((mine_ref, other_ref)):
        pltpu.make_async_copy(
            grad_ref.at[pl.ds(index * half, half)], out, out_sems.at[index]
        ).wait()


def per_device(tensor_blocks, block_coords, block_count, row_owner, factors, moment1, moment2):
    slot_count, edge, width = tensor_blocks.shape
    rank = factors.shape[2]
    local_blocks = moment1.shape[0] // edge
    row_blocks = row_owner.shape[1]
    dims = mesh_dims(lax.axis_size("blk"), lax.axis_size("grp"))
    shard = factors.astype(jnp.bfloat16).reshape(3 * local_blocks, edge, rank)
    peer = shift(jnp.concatenate([block_coords.reshape(-1), block_count]), dims, "core", 1)
    extra = shift(tensor_blocks, dims, "core", 1)
    pieces = gather_rows(shard, dims)
    smem = pl.BlockSpec(memory_space=pltpu.SMEM)
    hbm = pl.BlockSpec(memory_space=pl.ANY)
    tiles = edge // TILE_J
    outgoing = jax.ShapeDtypeStruct((row_blocks // 2, edge, rank), jnp.float32)
    mine, other = pl.pallas_call(
        functools.partial(slots_kernel, dims, local_blocks, len(pieces)),
        out_shape=(outgoing, outgoing),
        in_specs=[smem, smem, smem, smem, hbm, hbm] + [hbm] * len(pieces),
        out_specs=(hbm, hbm),
        scratch_shapes=[
            pltpu.VMEM((3 * row_blocks, edge, rank), jnp.bfloat16),
            pltpu.VMEM((row_blocks, edge, rank), jnp.float32),
            pltpu.VMEM((BUFFERS, edge, width), jnp.bfloat16),
            pltpu.VMEM((tiles, TILE_J * edge, rank), jnp.bfloat16),
            pltpu.VMEM((tiles, edge, TILE_J * edge), jnp.float32),
            pltpu.VMEM((edge, rank), jnp.float32),
            pltpu.SemaphoreType.DMA((BUFFERS, COPY_PARTS)),
            pltpu.SemaphoreType.DMA((len(pieces),)),
            pltpu.SemaphoreType.DMA((2,)),
        ],
        compiler_params=pltpu.CompilerParams(vmem_limit_bytes=56 * 1024 * 1024),
        cost_estimate=pl.CostEstimate(
            flops=4 * slot_count * edge * width * rank,
            bytes_accessed=2 * slot_count * edge * width,
            transcendentals=slot_count * edge * width,
        ),
    )(block_coords, block_count, row_owner, peer, tensor_blocks, extra, *pieces)

    def by_half(values):
        values = values.reshape(2, row_blocks // 4, edge, rank)
        out = []
        for half, (first, second) in enumerate(ORDERS):
            out.append(
                values[half].reshape(
                    dims[second], dims[first], dims["line"], local_blocks // 2 * edge, rank
                )
            )
        return out

    arrived = by_half(shift(other, dims, "core", 1))
    kept_halves = by_half(mine)
    sums = []
    for half, (first, second) in enumerate(ORDERS):
        kept, got = kept_halves[half], [arrived[half]]
        for name in (second, first):
            terms = [
                functools.reduce(jnp.add, [g[k] for g in got], kept[k]) for k in range(dims[name])
            ]
            kept = terms[0]
            got = [shift(terms[k], dims, name, k) for k in range(1, dims[name])]
        sums.append(functools.reduce(jnp.add, got, kept))
    rows = [jnp.concatenate([part[k] for part in sums]) for k in range(dims["line"])]
    grad = rows[0]
    for k in range(1, dims["line"]):
        grad = grad + shift(rows[k], dims, "line", k)
    new_moment1 = 0.9 * moment1 + 0.1 * grad
    new_moment2 = 0.999 * moment2 + 0.001 * grad * grad
    new_factor = factors[0] - 0.02 * (new_moment1 / (1.0 - 0.9**8)) / (
        jnp.sqrt(new_moment2 / (1.0 - 0.999**8)) + 1e-08
    )
    return (new_factor, new_moment1, new_moment2)


def solution(mesh):
    return jax.shard_map(
        per_device,
        mesh=mesh,
        in_specs=(
            P(AXES, None, None),
            P(None, AXES),
            P(AXES),
            P(),
            P(None, AXES, None),
            P(AXES, None),
            P(AXES, None),
        ),
        out_specs=(P(AXES, None), P(AXES, None), P(AXES, None)),
        check_vma=False,
    )
```
